128 devices in a mesh: path: 32 (over y, x, core), shard: 4 (over z).
Axes of the slice: x: 4, y: 4, z: 4, core: 2. Of those that a mesh axis runs over, the one named last changes fastest.
Arguments:
- path_table: int32 [32, 2], replicated, may hold values from 0 to 7, as said below
- master: float32 [16, 4096, 2048], P(None, 'path', 'shard'), may hold values from -0.09375 to 0.09375
- momentum: float32 [16, 4096, 2048], P(None, 'path', 'shard'), may hold values from -0.06 to 0.06
- deltas: bfloat16 [32, 2, 4096, 2048], P('path', None, None, 'shard'), may hold values from -0.059814453 to 0.059814453
- activations: bfloat16 [32768, 4096], P(('path', 'shard')), may hold values from -6 to 6
Outputs:
- new_master: float32 [16, 4096, 2048], P(None, 'path', 'shard')
- path_out: bfloat16 [32768, 4096], P(('path', 'shard'))
The draws below stay inside these ranges and needn't reach their ends.
Inputs may be any that keep to these rules, and one draw needn't show every extreme that they name: `path_table`: at every level each of the 8 choices is named by at least one path.
All inputs are finite; a program needn't handle non-finite values.
Results may differ from the reference program's by a relative error of at most 0.014.
Values may be sent and summed in bfloat16 or wider, within the bound.
A program may use at most 192 MiB of HBM per device.

```python
import jax
import jax.numpy as jnp
from jax import lax

D = 4096
HW = 2048
K = 8
LEV = 2
TOK = 1024
MODULES = 16
PATHS = 32
TOKENS = 32768
N_SHARD = 4


def draw_path_table(key, part):
    key = jax.random.fold_in(key, 7)
    columns = []
    for level in range(LEV):
        level_key = jax.random.fold_in(key, level)
        key_order, key_label, key_first, key_second = jax.random.split(level_key, 4)
        order = jax.random.permutation(key_order, PATHS)
        ranks = jnp.argsort(order, stable=True).astype(jnp.int32)
        labels = jax.random.permutation(key_label, K).astype(jnp.int32)
        skewed = jnp.minimum(jax.random.randint(key_first, (PATHS,), 0, K), jax.random.randint(key_second, (PATHS,), 0, K))
        choice_index = jnp.where(ranks < K, ranks, skewed)
        columns.append(labels[choice_index])
    return jnp.stack(columns, axis=1).astype(jnp.int32)


def block_levels(own_key, dims, shards, low, largest):
    def one(position, shards_of):
        draws = jax.random.uniform(jax.random.fold_in(jax.random.fold_in(own_key, 6), position), (shards_of,), jnp.float32, low / len(shards), largest / len(shards))
        return jnp.repeat(jnp.exp(draws), dims[position] // shards_of).reshape((-1,) + (1,) * (len(dims) - position - 1))

    gain = one(*shards[0])
    for cut in shards[1:]:
        gain = gain * one(*cut)
    return gain


def noise(rng, shape, spread, most, cuts=(), kind=jnp.bfloat16):
    values = spread * jax.random.normal(rng, shape, jnp.float32)
    if cuts:
        values = values * block_levels(rng, shape, cuts, -0.22, 0.18)
    return jnp.clip(values, -most, most).astype(kind)


def setup_inputs(seed: int = 0) -> dict:
    splits = jax.random.split(jax.random.key(seed), 6)
    return {
        "path_table": draw_path_table(jax.random.fold_in(splits[5], 71), 0),
        "master": noise(splits[1], (MODULES, D, HW), D ** -0.5, 0.09375, ((1, 32), (2, 4)), jnp.float32),
        "momentum": noise(splits[2], (MODULES, D, HW), 0.01, 0.06, ((1, 32), (2, 4)), jnp.float32),
        "deltas": noise(splits[3], (PATHS, LEV, D, HW), 0.01, 0.059814453, ((0, 32), (3, 4))),
        "activations": noise(splits[4], (TOKENS, D), 1.0, 6.0, ((0, 128),)),
    }


def reference(path_table, master, momentum, deltas, activations):
    module_of = path_table + (jnp.arange(LEV, dtype=jnp.int32) * K)[None, :]
    picks = jnp.arange(MODULES, dtype=jnp.int32)[:, None] == module_of.reshape(-1)[None, :]
    sums = jnp.dot(picks.astype(jnp.bfloat16), deltas.reshape(PATHS * LEV, D * HW), preferred_element_type=jnp.float32).reshape(MODULES, D, HW)
    counts = lax.optimization_barrier(jnp.sum(picks.astype(jnp.float32), axis=1))
    grad = sums / counts[:, None, None]
    new_momentum = 0.9 * momentum + grad
    new_master = master - 0.7 * (grad + 0.9 * new_momentum)
    fresh = new_master.astype(jnp.bfloat16)
    block = HW // N_SHARD

    def one_path(index):
        rows = lax.dynamic_slice_in_dim(activations, (index * TOK).astype(jnp.int32), TOK, 0)
        w_up = fresh[module_of[index, 0]]
        w_down = fresh[module_of[index, 1]]
        xf = rows.astype(jnp.float32)
        normed = (xf * lax.rsqrt(lax.optimization_barrier(jnp.mean(xf * xf, axis=1, keepdims=True)) + 1e-06)).astype(jnp.bfloat16)
        hidden = jax.nn.silu(jnp.dot(normed, w_up, preferred_element_type=jnp.float32)).astype(jnp.bfloat16)
        total = jnp.zeros((TOK, D), jnp.float32)
        for piece in range(N_SHARD):
            partial_value = lax.dot_general(hidden[:, piece * block:(piece + 1) * block], w_down[:, piece * block:(piece + 1) * block], (((1,), (1,)), ((), ())), preferred_element_type=jnp.float32)
            partial_value = lax.optimization_barrier(partial_value.astype(jnp.bfloat16))
            total = total + partial_value.astype(jnp.float32)
        return (xf + total).astype(jnp.bfloat16)
    outputs = lax.map(one_path, jnp.arange(PATHS, dtype=jnp.int32))
    return (new_master, outputs.reshape(TOKENS, D))
```

```python
import functools

import jax
import jax.numpy as jnp
from jax import lax
from jax.experimental import pallas as pl
from jax.experimental.pallas import tpu as pltpu
from jax.sharding import PartitionSpec as P

MESH = pl.DeviceIdType.MESH
F32 = jnp.float32
BF16 = jnp.bfloat16

TILE = 16
BIG = 32


def kernel(
    mods, wts, master, momentum, deltas, acts,
    nm_out, out,
    nrm, xbuf, xacc, mast, mom, rec0, rec1, fresh, wup, wdn, hid, parts,
    far_l, far_r, from_l, from_r,
    sem_a0, sem_a1, sem_b0, sem_b1,
    snd_a0, snd_a1, snd_b0, snd_b1,
    ag_snd, ag_l, ag_r, ag_f,
    rs_snd, rs_fl, rs_fr, rs_l, rs_r,
    sem_in, sem_out,
):
    n_path = rec0.shape[0]
    n_shard = nrm.shape[0]
    rows = rec0.shape[1]
    cols = rec0.shape[2]
    choices = fresh.shape[0]
    chunks0 = rows // BIG
    chunks1 = rows // TILE
    tokens = nrm.shape[1]
    half = tokens // 2
    me = lax.axis_index("path")
    z = lax.axis_index("shard")
    right = lax.rem(z + 1, n_shard)
    left = lax.rem(z + n_shard - 1, n_shard)

    def peer(i):
        j = lax.rem(i * 11, n_path)
        core = lax.rem(me + j, 2)
        x = lax.rem(me // 2 + j // 2, 4)
        y = lax.rem(me // 8 + j // 8, n_path // 8)
        return (y * 4 + x) * 2 + core

    load_x = pltpu.make_async_copy(acts, xbuf, sem_in.at[0])
    load_x.start()
    load_m = pltpu.make_async_copy(master, mast, sem_in.at[1])
    load_m.start()
    load_v = pltpu.make_async_copy(momentum, mom, sem_in.at[2])
    load_v.start()

    barrier = pltpu.get_barrier_semaphore()

    @pl.loop(1, n_path)
    def _(i):
        pl.semaphore_signal(barrier, inc=1, device_id={"path": peer(i)}, device_id_type=MESH)

    for side in (left, right):
        pl.semaphore_signal(barrier, inc=1, device_id={"shard": side}, device_id_type=MESH)
    pl.semaphore_wait(barrier, n_path - 1 + 2)

    def slice1(owner, c):
        return lax.rem(owner + c, chunks1)

    def send_a0(c):
        def src(q):
            return deltas.at[0, 0, pl.ds(pl.multiple_of(q * rows + c * BIG, BIG), BIG)]

        dst = rec0.at[me, pl.ds(c * BIG, BIG)]

        @pl.loop(1, n_path)
        def _(i):
            q = peer(i)
            pltpu.make_async_remote_copy(
                src(q), dst, snd_a0.at[c], sem_a0.at[c], device_id={"path": q}, device_id_type=MESH
            ).start()

        pltpu.make_async_copy(src(me), dst, sem_a0.at[c]).start()

    def send_a1(c):
        def src(q):
            return deltas.at[0, 1, pl.ds(pl.multiple_of(q * rows + slice1(q, c) * TILE, TILE), TILE)]

        dst = rec1.at[c, me]

        @pl.loop(1, n_path)
        def _(i):
            q = peer(i)
            pltpu.make_async_remote_copy(
                src(q), dst, snd_a1.at[c], sem_a1.at[c], device_id={"path": q}, device_id_type=MESH
            ).start()

        pltpu.make_async_copy(src(me), dst, sem_a1.at[c]).start()

    def send_b0(c):
        span = pl.ds(c * BIG, BIG)
        dst = wup.at[me, span]

        @pl.loop(1, n_path)
        def _(i):
            q = peer(i)
            pltpu.make_async_remote_copy(
                rec0.at[q, span], dst, snd_b0.at[c], sem_b0.at[c], device_id={"path": q}, device_id_type=MESH
            ).start()

        pltpu.make_async_copy(rec0.at[me, span], dst, sem_b0.at[c]).start()

    def send_b1(c):
        dst = wdn.at[c, (me // chunks1) * chunks1 + slice1(me, c)]

        @pl.loop(1, n_path)
        def _(i):
            q = peer(i)
            pltpu.make_async_remote_copy(
                rec1.at[c, q], dst, snd_b1.at[c], sem_b1.at[c], device_id={"path": q}, device_id_type=MESH
            ).start()

        pltpu.make_async_copy(rec1.at[c, me], dst, sem_b1.at[c]).start()

    def wait_like(ref, sem):
        pltpu.make_async_copy(ref, ref, sem).wait()

    def combine(level, take, put, state_row):
        at = pl.ds(state_row, TILE)
        width = 256
        for part in range(cols // width):
            lanes = pl.ds(part * width, width)

            def add(p, sums):
                value = take(p, lanes).astype(F32)
                return tuple(
                    total + wts[(level * n_path + p) * choices + m] * value for m, total in enumerate(sums)
                )

            grads = lax.fori_loop(
                0, n_path, add, tuple(jnp.zeros((TILE, width), F32) for _ in range(choices)), unroll=4
            )
            for m, grad in enumerate(grads):
                module = level * choices + m
                new_mom = 0.9 * mom[module, at, lanes] + grad
                new = mast[module, at, lanes] - 0.7 * (grad + 0.9 * new_mom)
                mast[module, at, lanes] = new
                fresh[m, :, lanes] = new.astype(BF16)

        @pl.loop(0, n_path, unroll=4)
        def _(p):
            put(p, fresh[mods[level * n_path + p]])

    def combine0(c):
        @pl.loop(0, BIG // TILE)
        def _(t):
            row = pl.multiple_of(c * BIG + t * TILE, TILE)

            def take(p, lanes):
                return rec0[p, pl.ds(row, TILE), lanes]

            def put(p, value):
                rec0[p, pl.ds(row, TILE), :] = value

            combine(0, take, put, row)

    def combine1(c):
        def take(p, lanes):
            return rec1[c, p, :, lanes]

        def put(p, value):
            rec1[c, p, :, :] = value

        combine(1, take, put, pl.multiple_of(slice1(me, c) * TILE, TILE))

    def z_copy(src, dst, send, recv, side):
        pltpu.make_async_remote_copy(
            src, dst, send, recv, device_id={"shard": side}, device_id_type=MESH
        ).start()

    for c in range(chunks0):
        send_a0(c)
    send_a1(0)
    send_a1(1)

    load_x.wait()

    @pl.loop(0, tokens // TILE)
    def _(t):
        at = pl.ds(pl.multiple_of(t * TILE, TILE), TILE)
        xf = xbuf[at, :].astype(F32)
        xacc[at, :] = xf
        scale = lax.rsqrt(jnp.mean(xf * xf, axis=1, keepdims=True) + 1e-06)
        nrm[z, at, :] = (xf * scale).astype(BF16)

    top, low = pl.ds(0, half), pl.ds(half, half)
    z_copy(nrm.at[z, top], nrm.at[z, top], ag_snd.at[0], ag_l.at[0], right)
    z_copy(nrm.at[z, low], nrm.at[z, low], ag_snd.at[1], ag_r.at[1], left)
    z_copy(nrm.at[z, low], nrm.at[z, low], ag_snd.at[2], ag_l.at[1], right)
    z_copy(nrm.at[z, top], nrm.at[z, top], ag_snd.at[3], ag_r.at[0], left)
    far = lax.rem(z + 2, n_shard)

    load_m.wait()
    load_v.wait()
    for c in range(chunks0):
        wait_like(rec0.at[:, pl.ds(c * BIG, BIG)], sem_a0.at[c])
        combine0(c)
        send_b0(c)
        if c == chunks0 - 2:
            wait_like(nrm.at[left, top], ag_l.at[0])
            z_copy(nrm.at[left, top], nrm.at[left, top], ag_snd.at[4], ag_f.at[0], right)
            wait_like(nrm.at[right, low], ag_r.at[1])
            z_copy(nrm.at[right, low], nrm.at[right, low], ag_snd.at[5], ag_f.at[1], left)
    state0 = pltpu.make_async_copy(mast.at[pl.ds(0, choices)], nm_out.at[pl.ds(0, choices)], sem_out.at[0])
    state0.start()

    def step_a1(c):
        wait_like(rec1.at[c], sem_a1.at[c])
        combine1(c)
        send_b1(c)
        if c + 2 < chunks1:
            send_a1(c + 2)

    def rs_first(c):
        wait_like(wdn.at[c], sem_b1.at[c])
        value = lax.dot_general(
            hid[...].reshape(n_shard * tokens, cols),
            wdn[c].reshape(n_path * TILE, cols),
            (((1,), (1,)), ((), ())),
            preferred_element_type=F32,
        ).astype(BF16)
        parts[c] = value.reshape(n_shard, tokens, n_path * TILE)
        z_copy(parts.at[c, 2, top], far_l.at[c], rs_snd.at[c], rs_fl.at[c], right)
        z_copy(parts.at[c, 2, low], far_r.at[c], rs_snd.at[c], rs_fr.at[c], left)
        z_copy(parts.at[c, 1, low], from_l.at[c, low], rs_snd.at[c], rs_l.at[c], right)
        z_copy(parts.at[c, 3, top], from_r.at[c, top], rs_snd.at[c], rs_r.at[c], left)

    def rs_second(c):
        wait_like(far_l.at[c], rs_fl.at[c])
        parts[c, 1, 0:half, :] = (parts[c, 1, 0:half, :].astype(F32) + far_l[c].astype(F32)).astype(BF16)
        z_copy(parts.at[c, 1, top], from_l.at[c, top], rs_snd.at[c], rs_l.at[c], right)
        wait_like(far_r.at[c], rs_fr.at[c])
        parts[c, 3, half:tokens, :] = (parts[c, 3, half:tokens, :].astype(F32) + far_r[c].astype(F32)).astype(BF16)
        z_copy(parts.at[c, 3, low], from_r.at[c, low], rs_snd.at[c], rs_r.at[c], left)

    def rs_last(c):
        wait_like(from_l.at[c], rs_l.at[c])
        wait_like(from_r.at[c], rs_r.at[c])
        group = lax.broadcasted_iota(jnp.int32, (TILE, 128), 1) // TILE

        @pl.loop(0, tokens // TILE)
        def _(t):
            at = pl.ds(pl.multiple_of(t * TILE, TILE), TILE)
            for g in range(n_path // chunks1):
                lanes = pl.ds(g * 128, 128)
                total = (
                    parts[c, 0, at, lanes].astype(F32)
                    + from_l[c, at, lanes].astype(F32)
                    + from_r[c, at, lanes].astype(F32)
                )
                for q in range(chunks1):
                    lane = pl.ds((g * chunks1 + q) * 128, 128)
                    value = xacc[at, lane] + jnp.where(group == (c + q) % chunks1, total, 0.0)
                    if c == chunks1 - 1:
                        out[at, lane] = value.astype(BF16)
                    else:
                        xacc[at, lane] = value

    step_a1(0)
    step_a1(1)

    wait_like(nrm.at[left, low], ag_l.at[1])
    wait_like(nrm.at[right, top], ag_r.at[0])
    wait_like(nrm.at[far, top], ag_f.at[0])
    wait_like(nrm.at[far, low], ag_f.at[1])
    for c in range(chunks0):
        wait_like(wup.at[:, pl.ds(c * BIG, BIG)], sem_b0.at[c])

    @pl.loop(0, n_shard)
    def _(d):
        value = jnp.dot(
            nrm[lax.rem(z + d, n_shard)], wup[...].reshape(n_path * rows, cols), preferred_element_type=F32
        )
        hid[d] = (value / (1.0 + jnp.exp(-value))).astype(BF16)

    for c in range(chunks1):
        rs_first(c)
        if c >= 1:
            rs_second(c - 1)
        if c >= 2:
            rs_last(c - 2)
        if c + 2 < chunks1:
            step_a1(c + 2)
        if c + 2 == chunks1 - 1:
            state1 = pltpu.make_async_copy(
                mast.at[pl.ds(choices, choices)], nm_out.at[pl.ds(choices, choices)], sem_out.at[1]
            )
            state1.start()
    rs_second(chunks1 - 1)
    rs_last(chunks1 - 2)
    rs_last(chunks1 - 1)

    others = pl.ds(0, n_path - 1)
    for c in range(chunks0):
        wait_like(rec0.at[others, pl.ds(c * BIG, BIG)], snd_a0.at[c])
        wait_like(rec0.at[others, pl.ds(c * BIG, BIG)], snd_b0.at[c])
    for c in range(chunks1):
        wait_like(rec1.at[c, others], snd_a1.at[c])
        wait_like(rec1.at[c, others], snd_b1.at[c])
        wait_like(parts.at[c, pl.ds(0, 3)], rs_snd.at[c])
    for k in range(6):
        wait_like(nrm.at[0, top], ag_snd.at[k])
    state0.wait()
    state1.wait()


def per_device(path_table, master, momentum, deltas, activations):
    n_path = lax.axis_size("path")
    n_shard = lax.axis_size("shard")
    levels = deltas.shape[1]
    modules, rows, cols = master.shape
    choices = modules // levels
    tokens, width = activations.shape
    chunks0, chunks1 = rows // BIG, rows // TILE
    table = path_table.T
    picks = (table[:, :, None] == jnp.arange(choices, dtype=jnp.int32)[None, None, :]).astype(F32)
    wts = picks / jnp.sum(picks, axis=1, keepdims=True)
    hbm = pl.BlockSpec(memory_space=pl.ANY)
    smem = pl.BlockSpec(memory_space=pltpu.SMEM)
    dma = pltpu.SemaphoreType.DMA
    block = n_path * TILE
    return tuple(pl.pallas_call(
        kernel,
        out_shape=(
            jax.ShapeDtypeStruct((modules, rows, cols), F32),
            jax.ShapeDtypeStruct((tokens, width), BF16),
        ),
        in_specs=[smem, smem, hbm, hbm, hbm, hbm],
        out_specs=(hbm, pl.BlockSpec(memory_space=pltpu.VMEM)),
        scratch_shapes=[
            pltpu.VMEM((n_shard, tokens, width), BF16),
            pltpu.VMEM((tokens, width), BF16),
            pltpu.VMEM((tokens, width), F32),
            pltpu.VMEM((modules, rows, cols), F32),
            pltpu.VMEM((modules, rows, cols), F32),
            pltpu.VMEM((n_path, rows, cols), BF16),
            pltpu.VMEM((chunks1, n_path, TILE, cols), BF16),
            pltpu.VMEM((choices, TILE, cols), BF16),
            pltpu.VMEM((n_path, rows, cols), BF16),
            pltpu.VMEM((chunks1, n_path, TILE, cols), BF16),
            pltpu.VMEM((n_shard, tokens, cols), BF16),
            pltpu.VMEM((chunks1, n_shard, tokens, block), BF16),
            pltpu.VMEM((chunks1, tokens // 2, block), BF16),
            pltpu.VMEM((chunks1, tokens // 2, block), BF16),
            pltpu.VMEM((chunks1, tokens, block), BF16),
            pltpu.VMEM((chunks1, tokens, block), BF16),
            dma((chunks0,)), dma((chunks1,)), dma((chunks0,)), dma((chunks1,)),
            dma((chunks0,)), dma((chunks1,)), dma((chunks0,)), dma((chunks1,)),
            dma((6,)), dma((2,)), dma((2,)), dma((2,)),
            dma((chunks1,)), dma((chunks1,)), dma((chunks1,)), dma((chunks1,)), dma((chunks1,)),
            dma((3,)), dma((2,)),
        ],
        compiler_params=pltpu.CompilerParams(
            collective_id=0, has_side_effects=True, vmem_limit_bytes=62 * 1024 * 1024
        ),
    )(table.reshape(-1), wts.reshape(-1), master, momentum, deltas, activations))


def solution(mesh):
    placed = (
        P(),
        P(None, "path", "shard"),
        P(None, "path", "shard"),
        P("path", None, None, "shard"),
        P(("path", "shard"), None),
    )
    return jax.shard_map(
        per_device,
        mesh=mesh,
        in_specs=placed,
        out_specs=(P(None, "path", "shard"), P(("path", "shard"), None)),
        check_vma=False,
    )
```

```python
import jax
import jax.numpy as jnp
from jax import lax
from jax.experimental import pallas as pl
from jax.experimental.pallas import tpu as pltpu
from jax.sharding import PartitionSpec as P

MESH = pl.DeviceIdType.MESH
F32 = jnp.float32
BF16 = jnp.bfloat16

TILE = 16
SLOTS = 4
AHEAD = 3
SIDE = 4


def kernel(
    table, master, momentum, deltas, acts,
    state, out,
    wts, counts,
    nrm, momb, rec, part, far, frm, dense, pick, wup, wdn, hid, rs_far, rs_frm,
    s_a, s_far, s_frm, s_bi, s_bf, s_b,
    o_a, o_p, o_bi, o_b,
    ag_snd, ag_l, ag_r, ag_f,
    rs_snd, s_rfar, s_rfrm,
    sem_in, sem_mom,
):
    levels = deltas.shape[0]
    rows = deltas.shape[4]
    cols = deltas.shape[5]
    jobs = rec.shape[0]
    per_level = jobs // levels
    choices = dense.shape[3]
    group = rec.shape[2]
    n_path = SIDE * group
    n_shard, tokens, width = nrm.shape
    half = tokens // 2
    some = choices // 2
    lanes_of = [pl.ds(t * (cols // 2), cols // 2) for t in range(2)]
    block = n_path * TILE

    me = lax.axis_index("path")
    z = lax.axis_index("shard")
    core = lax.rem(me, 2)
    x = lax.rem(me // 2, SIDE)
    y = me // group
    right = lax.rem(z + 1, n_shard)
    left = lax.rem(z + n_shard - 1, n_shard)
    direct = (y, x)
    ring = (x, y)

    def path_of(t, d, r, c):
        return (d * SIDE + r) * 2 + c if t == 0 else (r * SIDE + d) * 2 + c

    def member(t, s):
        return path_of(t, s // 2, ring[t], s % 2)

    def offset(i):
        return lax.rem(i * 3, group)

    def direct_slot(t, i):
        j = offset(i)
        return lax.rem(direct[t] + j // 2, SIDE) * 2 + lax.rem(core + j, 2)

    def direct_peer(t, slot):
        return path_of(t, slot // 2, ring[t], lax.rem(slot, 2))

    ring_up = [path_of(t, direct[t], lax.rem(ring[t] + 1, SIDE), core) for t in range(2)]
    ring_down = [path_of(t, direct[t], lax.rem(ring[t] + SIDE - 1, SIDE), core) for t in range(2)]

    load_x = pltpu.make_async_copy(acts, out, sem_in.at[0])
    load_x.start()
    load_m = pltpu.make_async_copy(master, state, sem_in.at[1])
    load_m.start()

    barrier = pltpu.get_barrier_semaphore()

    @pl.loop(1, group)
    def _(i):
        slot = direct_slot(0, i)
        pl.semaphore_signal(barrier, inc=1, device_id={"path": direct_peer(0, slot)}, device_id_type=MESH)

    @pl.loop(2, group)
    def _(i):
        slot = lax.rem(direct[1] + i // 2, SIDE) * 2 + lax.rem(core + i, 2)
        pl.semaphore_signal(barrier, inc=1, device_id={"path": direct_peer(1, slot)}, device_id_type=MESH)

    for side in (left, right):
        pl.semaphore_signal(barrier, inc=1, device_id={"shard": side}, device_id_type=MESH)
    pl.semaphore_wait(barrier, (group - 1) + (group - 2) + 2)

    def wait_like(ref, sem):
        pltpu.make_async_copy(ref, ref, sem).wait()

    def p_copy(src, dst, send, recv, peer):
        pltpu.make_async_remote_copy(
            src, dst, send, recv, device_id={"path": peer}, device_id_type=MESH
        ).start()

    def z_copy(src, dst, send, recv, side):
        pltpu.make_async_remote_copy(
            src, dst, send, recv, device_id={"shard": side}, device_id_type=MESH
        ).start()

    def rows_of(j):
        return pl.ds(pl.multiple_of(lax.rem(j, per_level) * TILE, TILE), TILE)

    def send_deltas(j):
        level = j // per_level
        at = rows_of(j)

        def src(t, slot):
            d, c = slot // 2, lax.rem(slot, 2)
            if t == 0:
                return deltas.at[level, d, :, c, at, lanes_of[0]]
            return deltas.at[level, :, d, c, at, lanes_of[1]]

        def dst(t):
            return rec.at[j, t, direct[t] * 2 + core]

        @pl.loop(1, group)
        def _(i):
            for t in range(2):
                slot = direct_slot(t, i)
                p_copy(src(t, slot), dst(t), o_a.at[0], s_a.at[j, t], direct_peer(t, slot))

        for t in range(2):
            pltpu.make_async_copy(src(t, direct[t] * 2 + core), dst(t), s_a.at[j, t]).start()

    def sums(j, t, owner):
        base = (j // per_level) * n_path
        total = [None] * choices
        for s in range(group):
            value = rec[j, t, s, owner].astype(F32)
            at = (base + member(t, s)) * choices
            for m in range(choices):
                term = wts[at + m] * value
                total[m] = term if total[m] is None else total[m] + term
        return total

    def momentum_copy(j):
        level = j // per_level
        slot = lax.rem(j, SLOTS)
        return pltpu.make_async_copy(
            momentum.at[pl.ds(level * choices, choices), rows_of(j)], momb.at[slot], sem_mom.at[slot]
        )

    first, second = pl.ds(0, some), pl.ds(some, some)

    def step1(j):
        slot = lax.rem(j, SLOTS)

        @pl.when(j >= SLOTS)
        def _():
            wait_like(part.at[slot], o_p.at[j - SLOTS])

        momentum_copy(j).start()
        for t in range(2):
            wait_like(rec.at[j, t], s_a.at[j, t])

        def fill(t, k):
            for m, value in enumerate(sums(j, t, lax.rem(ring[t] + k, SIDE))):
                part[slot, t, k - 1, m] = value.astype(BF16)

        for t in range(2):
            fill(t, 2)
            p_copy(part.at[slot, t, 1, first], far.at[j, t, 0], o_p.at[j], s_far.at[j, t, 0], ring_up[t])
            p_copy(part.at[slot, t, 1, second], far.at[j, t, 1], o_p.at[j], s_far.at[j, t, 1], ring_down[t])
        for t in range(2):
            fill(t, 1)
            p_copy(part.at[slot, t, 0, second], frm.at[j, t, 0, second], o_p.at[j], s_frm.at[j, t, 0], ring_up[t])
            fill(t, 3)
            p_copy(part.at[slot, t, 2, first], frm.at[j, t, 1, first], o_p.at[j], s_frm.at[j, t, 1], ring_down[t])

    def step2(j):
        slot = lax.rem(j, SLOTS)
        for t in range(2):
            wait_like(far.at[j, t, 0], s_far.at[j, t, 0])
            for m in range(some):
                part[slot, t, 0, m] = (part[slot, t, 0, m].astype(F32) + far[j, t, 0, m].astype(F32)).astype(BF16)
            p_copy(part.at[slot, t, 0, first], frm.at[j, t, 0, first], o_p.at[j], s_frm.at[j, t, 0], ring_up[t])
            wait_like(far.at[j, t, 1], s_far.at[j, t, 1])
            for m in range(some):
                n = some + m
                part[slot, t, 2, n] = (part[slot, t, 2, n].astype(F32) + far[j, t, 1, m].astype(F32)).astype(BF16)
            p_copy(part.at[slot, t, 2, second], frm.at[j, t, 1, second], o_p.at[j], s_frm.at[j, t, 1], ring_down[t])

    def step3(j):
        level = j // per_level
        slot = lax.rem(j, SLOTS)
        at = rows_of(j)
        momentum_copy(j).wait()
        for t in range(2):
            wait_like(frm.at[j, t, 0], s_frm.at[j, t, 0])
            wait_like(frm.at[j, t, 1], s_frm.at[j, t, 1])
            for m, total in enumerate(sums(j, t, ring[t])):
                module = level * choices + m
                total = total + frm[j, t, 0, m].astype(F32) + frm[j, t, 1, m].astype(F32)
                grad = total / jnp.full(total.shape, counts[module], F32)
                new_mom = 0.9 * momb[slot, m, :, lanes_of[t]] + grad
                new = state[module, at, lanes_of[t]] - 0.7 * (grad + 0.9 * new_mom)
                state[module, at, lanes_of[t]] = new
                dense[j, t, 0, m] = new.astype(BF16)
            own = dense.at[j, t, 0]
            p_copy(own.at[first], dense.at[j, t, 3, first], o_bi.at[0], s_bf.at[j, t, 0], ring_up[t])
            p_copy(own.at[second], dense.at[j, t, 1, second], o_bi.at[0], s_bf.at[j, t, 1], ring_down[t])
            p_copy(own.at[second], dense.at[j, t, 3, second], o_bi.at[0], s_bi.at[j, t], ring_up[t])
            p_copy(own.at[first], dense.at[j, t, 1, first], o_bi.at[0], s_bi.at[j, t], ring_down[t])

    def step4(j):
        for t in range(2):
            wait_like(dense.at[j, t, 3, first], s_bf.at[j, t, 0])
            p_copy(dense.at[j, t, 3, first], dense.at[j, t, 2, first], o_bi.at[0], s_bi.at[j, t], ring_up[t])
            wait_like(dense.at[j, t, 1, second], s_bf.at[j, t, 1])
            p_copy(dense.at[j, t, 1, second], dense.at[j, t, 2, second], o_bi.at[0], s_bi.at[j, t], ring_down[t])

    def step5(j):
        level = j // per_level
        at = rows_of(j)
        chunk = lax.rem(j, per_level)
        for t in range(2):
            wait_like(dense.at[j, t, pl.ds(0, 2)], s_bi.at[j, t])
            for k in range(SIDE):
                pick[t, k] = dense[j, t, k]

            @pl.loop(0, group)
            def _(s):
                need = table[level, direct_peer(t, s)]
                for k in range(SIDE):
                    rec[j, t, s, lax.rem(ring[t] + k, SIDE)] = pick[t, k, need]

        def send(dst):
            @pl.loop(1, group)
            def _(i):
                for t in range(2):
                    slot = direct_slot(t, i)
                    p_copy(rec.at[j, t, slot], dst(t), o_b.at[0], s_b.at[j, t], direct_peer(t, slot))

            for t in range(2):
                pltpu.make_async_copy(rec.at[j, t, direct[t] * 2 + core], dst(t), s_b.at[j, t]).start()

        @pl.when(level == 0)
        def _():
            def dst(t):
                if t == 0:
                    return wup.at[y, :, core, at, lanes_of[0]]
                return wup.at[:, x, core, at, lanes_of[1]]

            send(dst)

        @pl.when(level == 1)
        def _():
            def dst(t):
                if t == 0:
                    return wdn.at[chunk, y, :, core, :, lanes_of[0]]
                return wdn.at[chunk, :, x, core, :, lanes_of[1]]

            send(dst)

    top, low = pl.ds(0, half), pl.ds(half, half)
    opposite = lax.rem(z + 2, n_shard)

    def first_projection():
        wait_like(nrm.at[left, low], ag_l.at[1])
        wait_like(nrm.at[right, top], ag_r.at[0])
        wait_like(nrm.at[opposite, top], ag_f.at[0])
        wait_like(nrm.at[opposite, low], ag_f.at[1])
        wait_like(nrm.at[pl.ds(0, 3)], ag_snd.at[0])

        @pl.loop(0, n_shard)
        def _(d):
            value = jnp.dot(
                nrm[lax.rem(z + d, n_shard)], wup[...].reshape(n_path * rows, cols), preferred_element_type=F32
            )
            hid[d] = (value / (1.0 + jnp.exp(-value))).astype(BF16)

    def features(c):
        return pl.ds(pl.multiple_of(c * block, block), block)

    def rs_first(c):
        at = features(c)
        value = lax.dot_general(
            hid[...].reshape(n_shard * tokens, cols),
            wdn[c].reshape(block, cols),
            (((1,), (1,)), ((), ())),
            preferred_element_type=F32,
        ).astype(BF16)
        nrm[:, :, at] = value.reshape(n_shard, tokens, block)
        z_copy(nrm.at[2, top, at], rs_far.at[c, 0], rs_snd.at[0], s_rfar.at[c, 0], right)
        z_copy(nrm.at[2, low, at], rs_far.at[c, 1], rs_snd.at[0], s_rfar.at[c, 1], left)
        z_copy(nrm.at[1, low, at], rs_frm.at[c, 0, low], rs_snd.at[0], s_rfrm.at[c, 0], right)
        z_copy(nrm.at[3, top, at], rs_frm.at[c, 1, top], rs_snd.at[0], s_rfrm.at[c, 1], left)

    def rs_second(c):
        at = features(c)
        wait_like(rs_far.at[c, 0], s_rfar.at[c, 0])
        nrm[1, 0:half, at] = (nrm[1, 0:half, at].astype(F32) + rs_far[c, 0].astype(F32)).astype(BF16)
        z_copy(nrm.at[1, top, at], rs_frm.at[c, 0, top], rs_snd.at[0], s_rfrm.at[c, 0], right)
        wait_like(rs_far.at[c, 1], s_rfar.at[c, 1])
        nrm[3, half:tokens, at] = (nrm[3, half:tokens, at].astype(F32) + rs_far[c, 1].astype(F32)).astype(BF16)
        z_copy(nrm.at[3, low, at], rs_frm.at[c, 1, low], rs_snd.at[0], s_rfrm.at[c, 1], left)

    def rs_last(c):
        wait_like(rs_frm.at[c, 0], s_rfrm.at[c, 0])
        wait_like(rs_frm.at[c, 1], s_rfrm.at[c, 1])
        fit = lax.broadcasted_iota(jnp.int32, (TILE, 128), 1) // TILE == c
        per = 128 // TILE

        @pl.loop(0, tokens // TILE)
        def _(i):
            at = pl.ds(pl.multiple_of(i * TILE, TILE), TILE)
            for g in range(block // 128):
                lanes = pl.ds(g * 128, 128)
                total = (
                    nrm[0, at, pl.ds(pl.multiple_of(c * block + g * 128, 128), 128)].astype(F32)
                    + rs_frm[c, 0, at, lanes].astype(F32)
                    + rs_frm[c, 1, at, lanes].astype(F32)
                )
                for q in range(per):
                    place = pl.ds((g * per + q) * 128, 128)
                    moved = pltpu.roll(total, lax.rem(c + per - q, per) * TILE, 1)
                    old = out[at, place].astype(F32)
                    out[at, place] = jnp.where(fit, old + moved, old).astype(BF16)

    for j in range(AHEAD):
        send_deltas(j)

    @pl.loop(0, levels)
    def _(level):
        for m in range(choices):
            def count(p, total):
                named = jnp.where(table[level, p] == m, 1.0, 0.0)
                wts[(level * n_path + p) * choices + m] = named
                return total + named

            counts[level * choices + m] = lax.fori_loop(0, n_path, count, jnp.float32(0.0))

    load_x.wait()

    @pl.loop(0, tokens // TILE)
    def _(i):
        at = pl.ds(pl.multiple_of(i * TILE, TILE), TILE)
        xf = out[at, :].astype(F32)
        scale = lax.rsqrt(jnp.mean(xf * xf, axis=1, keepdims=True) + 1e-06)
        nrm[z, at, :] = (xf * scale).astype(BF16)

    z_copy(nrm.at[z, top], nrm.at[z, top], ag_snd.at[0], ag_l.at[0], right)
    z_copy(nrm.at[z, low], nrm.at[z, low], ag_snd.at[0], ag_r.at[1], left)
    z_copy(nrm.at[z, low], nrm.at[z, low], ag_snd.at[0], ag_l.at[1], right)
    z_copy(nrm.at[z, top], nrm.at[z, top], ag_snd.at[0], ag_r.at[0], left)
    load_m.wait()

    @pl.loop(0, jobs + 3)
    def _(n):
        def when(low_job, job, high_job, *steps):
            @pl.when((job >= low_job) & (job < high_job))
            def _():
                for step in steps:
                    step()

        when(0, n, jobs, lambda: step1(n))
        when(0, n + AHEAD, jobs, lambda: send_deltas(n + AHEAD))
        when(0, n - 1, jobs, lambda: step3(n - 1))
        when(0, n - 2, jobs, lambda: step5(n - 2))
        when(per_level, n - 3, jobs, lambda: rs_second(n - 3 - per_level))
        when(0, n, jobs, lambda: step2(n))
        when(0, n - 1, jobs, lambda: step4(n - 1))

        @pl.when(n == 4)
        def _():
            wait_like(nrm.at[left, top], ag_l.at[0])
            z_copy(nrm.at[left, top], nrm.at[left, top], ag_snd.at[0], ag_f.at[0], right)
            wait_like(nrm.at[right, low], ag_r.at[1])
            z_copy(nrm.at[right, low], nrm.at[right, low], ag_snd.at[0], ag_f.at[1], left)

        def arrived():
            for t in range(2):
                wait_like(rec.at[n - 2, t], s_b.at[n - 2, t])

        when(0, n - 2, jobs, arrived)
        when(per_level - 1, n - 2, per_level, first_projection)
        when(per_level, n - 2, jobs, lambda: rs_first(n - 2 - per_level))
        when(per_level, n - 3, jobs, lambda: rs_last(n - 3 - per_level))

    others = pl.ds(0, group - 1)
    wait_like(rec.at[:, :, others], o_a.at[0])
    wait_like(rec.at[:, :, others], o_b.at[0])
    wait_like(dense.at[:, :, pl.ds(0, 3)], o_bi.at[0])
    for j in range(jobs - SLOTS, jobs):
        wait_like(part.at[j % SLOTS], o_p.at[j])
    wait_like(nrm.at[pl.ds(0, 3)], rs_snd.at[0])


def per_device(path_table, master, momentum, deltas, activations):
    n_path = lax.axis_size("path")
    n_shard = lax.axis_size("shard")
    levels = deltas.shape[1]
    modules, rows, cols = master.shape
    choices = modules // levels
    tokens, width = activations.shape
    group = n_path // SIDE
    per_level = rows // TILE
    jobs = levels * per_level
    hbm = pl.BlockSpec(memory_space=pl.ANY)
    vmem = pl.BlockSpec(memory_space=pltpu.VMEM)
    smem = pl.BlockSpec(memory_space=pltpu.SMEM)
    dma = pltpu.SemaphoreType.DMA
    block = n_path * TILE
    wide = cols // 2
    return tuple(pl.pallas_call(
        kernel,
        out_shape=(
            jax.ShapeDtypeStruct((modules, rows, cols), F32),
            jax.ShapeDtypeStruct((tokens, width), BF16),
        ),
        in_specs=[smem, hbm, hbm, hbm, hbm],
        out_specs=(vmem, vmem),
        scratch_shapes=[
            pltpu.SMEM((levels * n_path * choices,), F32),
            pltpu.SMEM((modules,), F32),
            pltpu.VMEM((n_shard, tokens, width), BF16),
            pltpu.VMEM((SLOTS, choices, TILE, cols), F32),
            pltpu.VMEM((jobs, 2, group, SIDE, TILE, wide), BF16),
            pltpu.VMEM((SLOTS, 2, 3, choices, TILE, wide), BF16),
            pltpu.VMEM((jobs, 2, 2, choices // 2, TILE, wide), BF16),
            pltpu.VMEM((jobs, 2, 2, choices, TILE, wide), BF16),
            pltpu.VMEM((jobs, 2, SIDE, choices, TILE, wide), BF16),
            pltpu.VMEM((2, SIDE, choices, TILE, wide), BF16),
            pltpu.VMEM((SIDE, SIDE, 2, rows, cols), BF16),
            pltpu.VMEM((per_level, SIDE, SIDE, 2, TILE, cols), BF16),
            pltpu.VMEM((n_shard, tokens, cols), BF16),
            pltpu.VMEM((per_level, 2, tokens // 2, block), BF16),
            pltpu.VMEM((per_level, 2, tokens, block), BF16),
            dma((jobs, 2)), dma((jobs, 2, 2)), dma((jobs, 2, 2)), dma((jobs, 2)), dma((jobs, 2, 2)), dma((jobs, 2)),
            dma((1,)), dma((jobs,)), dma((1,)), dma((1,)),
            dma((1,)), dma((2,)), dma((2,)), dma((2,)),
            dma((1,)), dma((per_level, 2)), dma((per_level, 2)),
            dma((2,)), dma((SLOTS,)),
        ],
        compiler_params=pltpu.CompilerParams(
            collective_id=0, has_side_effects=True, vmem_limit_bytes=62 * 1024 * 1024
        ),
    )(
        path_table.T,
        master,
        momentum,
        deltas.reshape(levels, SIDE, SIDE, 2, rows, cols),
        activations,
    ))


def solution(mesh):
    placed = (
        P(),
        P(None, "path", "shard"),
        P(None, "path", "shard"),
        P("path", None, None, "shard"),
        P(("path", "shard"), None),
    )
    return jax.shard_map(
        per_device,
        mesh=mesh,
        in_specs=placed,
        out_specs=(P(None, "path", "shard"), P(("path", "shard"), None)),
        check_vma=False,
    )
```

```python
import jax
import jax.numpy as jnp
from jax import lax
from jax.experimental import pallas as pl
from jax.experimental.pallas import tpu as pltpu
from jax.sharding import PartitionSpec as P

MESH = pl.DeviceIdType.MESH
F32 = jnp.float32
BF16 = jnp.bfloat16

TILE = 16
SLOTS = 4
AHEAD = 2
SIDE = 4


def kernel(
    table, master, momentum, deltas, acts,
    state, out,
    wts, counts,
    nrm, momb, rec, part, far, frm, dense, pick, wup, wdn, hid, rs_far, rs_frm,
    s_a, s_far, s_frm, s_bi, s_bf, s_b,
    o_a, o_p, o_bi, o_b,
    ag_snd, ag_l, ag_r, ag_f,
    rs_snd, s_rfar, s_rfrm,
    sem_in, sem_mom,
):
    levels = deltas.shape[0]
    rows = deltas.shape[4]
    cols = deltas.shape[5]
    jobs = rec.shape[0]
    per_level = jobs // levels
    choices = dense.shape[3]
    group = rec.shape[2]
    n_path = SIDE * group
    n_shard, tokens, width = nrm.shape
    half = tokens // 2
    some = choices // 2
    lanes_of = [pl.ds(t * (cols // 2), cols // 2) for t in range(2)]
    block = n_path * TILE

    me = lax.axis_index("path")
    z = lax.axis_index("shard")
    core = lax.rem(me, 2)
    x = lax.rem(me // 2, SIDE)
    y = me // group
    right = lax.rem(z + 1, n_shard)
    left = lax.rem(z + n_shard - 1, n_shard)
    direct = (y, x)
    ring = (x, y)

    def path_of(t, d, r, c):
        return (d * SIDE + r) * 2 + c if t == 0 else (r * SIDE + d) * 2 + c

    def member(t, s):
        return path_of(t, s // 2, ring[t], s % 2)

    def offset(i):
        return lax.rem(i * 3, group)

    def direct_slot(t, i):
        j = offset(i)
        return lax.rem(direct[t] + j // 2, SIDE) * 2 + lax.rem(core + j, 2)

    def direct_peer(t, slot):
        return path_of(t, slot // 2, ring[t], lax.rem(slot, 2))

    ring_up = [path_of(t, direct[t], lax.rem(ring[t] + 1, SIDE), core) for t in range(2)]
    ring_down = [path_of(t, direct[t], lax.rem(ring[t] + SIDE - 1, SIDE), core) for t in range(2)]

    load_x = pltpu.make_async_copy(acts, out, sem_in.at[0])
    load_x.start()
    load_m = pltpu.make_async_copy(master, state, sem_in.at[1])
    load_m.start()

    barrier = pltpu.get_barrier_semaphore()

    @pl.loop(1, group)
    def _(i):
        slot = direct_slot(0, i)
        pl.semaphore_signal(barrier, inc=1, device_id={"path": direct_peer(0, slot)}, device_id_type=MESH)

    @pl.loop(2, group)
    def _(i):
        slot = lax.rem(direct[1] + i // 2, SIDE) * 2 + lax.rem(core + i, 2)
        pl.semaphore_signal(barrier, inc=1, device_id={"path": direct_peer(1, slot)}, device_id_type=MESH)

    for side in (left, right):
        pl.semaphore_signal(barrier, inc=1, device_id={"shard": side}, device_id_type=MESH)
    pl.semaphore_wait(barrier, (group - 1) + (group - 2) + 2)

    def wait_like(ref, sem):
        pltpu.make_async_copy(ref, ref, sem).wait()

    def p_copy(src, dst, send, recv, peer):
        pltpu.make_async_remote_copy(
            src, dst, send, recv, device_id={"path": peer}, device_id_type=MESH
        ).start()

    def z_copy(src, dst, send, recv, side):
        pltpu.make_async_remote_copy(
            src, dst, send, recv, device_id={"shard": side}, device_id_type=MESH
        ).start()

    def rows_of(j):
        return pl.ds(pl.multiple_of(lax.rem(j, per_level) * TILE, TILE), TILE)

    def send_deltas(j):
        level = j // per_level
        at = rows_of(j)

        def src(t, slot):
            d, c = slot // 2, lax.rem(slot, 2)
            if t == 0:
                return deltas.at[level, d, :, c, at, lanes_of[0]]
            return deltas.at[level, :, d, c, at, lanes_of[1]]

        def dst(t):
            return rec.at[j, t, direct[t] * 2 + core]

        @pl.loop(1, group)
        def _(i):
            for t in range(2):
                slot = direct_slot(t, i)
                p_copy(src(t, slot), dst(t), o_a.at[0], s_a.at[j, t], direct_peer(t, slot))

        for t in range(2):
            pltpu.make_async_copy(src(t, direct[t] * 2 + core), dst(t), s_a.at[j, t]).start()

    def sums(j, t, owner):
        base = (j // per_level) * n_path
        total = [None] * choices
        for s in range(group):
            value = rec[j, t, s, owner].astype(F32)
            at = (base + member(t, s)) * choices
            for m in range(choices):
                term = wts[at + m] * value
                total[m] = term if total[m] is None else total[m] + term
        return total

    def momentum_copy(j):
        level = j // per_level
        slot = lax.rem(j, SLOTS)
        return pltpu.make_async_copy(
            momentum.at[pl.ds(level * choices, choices), rows_of(j)], momb.at[slot], sem_mom.at[slot]
        )

    first, second = pl.ds(0, some), pl.ds(some, some)

    def step1(j):
        slot = lax.rem(j, SLOTS)

        @pl.when(j >= SLOTS)
        def _():
            wait_like(part.at[slot], o_p.at[j - SLOTS])

        momentum_copy(j).start()
        for t in range(2):
            wait_like(rec.at[j, t], s_a.at[j, t])

        def fill(t, k):
            for m, value in enumerate(sums(j, t, lax.rem(ring[t] + k, SIDE))):
                part[slot, t, k - 1, m] = value.astype(BF16)

        for t in range(2):
            fill(t, 2)
            p_copy(part.at[slot, t, 1, first], far.at[j, t, 0], o_p.at[j], s_far.at[j, t, 0], ring_up[t])
            p_copy(part.at[slot, t, 1, second], far.at[j, t, 1], o_p.at[j], s_far.at[j, t, 1], ring_down[t])
        for t in range(2):
            fill(t, 1)
            p_copy(part.at[slot, t, 0, second], frm.at[j, t, 0, second], o_p.at[j], s_frm.at[j, t, 0], ring_up[t])
            fill(t, 3)
            p_copy(part.at[slot, t, 2, first], frm.at[j, t, 1, first], o_p.at[j], s_frm.at[j, t, 1], ring_down[t])

    def step2(j):
        slot = lax.rem(j, SLOTS)
        for t in range(2):
            wait_like(far.at[j, t, 0], s_far.at[j, t, 0])
            for m in range(some):
                part[slot, t, 0, m] = (part[slot, t, 0, m].astype(F32) + far[j, t, 0, m].astype(F32)).astype(BF16)
            p_copy(part.at[slot, t, 0, first], frm.at[j, t, 0, first], o_p.at[j], s_frm.at[j, t, 0], ring_up[t])
            wait_like(far.at[j, t, 1], s_far.at[j, t, 1])
            for m in range(some):
                n = some + m
                part[slot, t, 2, n] = (part[slot, t, 2, n].astype(F32) + far[j, t, 1, m].astype(F32)).astype(BF16)
            p_copy(part.at[slot, t, 2, second], frm.at[j, t, 1, second], o_p.at[j], s_frm.at[j, t, 1], ring_down[t])

    def step3(j):
        level = j // per_level
        slot = lax.rem(j, SLOTS)
        at = rows_of(j)
        momentum_copy(j).wait()
        for t in range(2):
            wait_like(frm.at[j, t, 0], s_frm.at[j, t, 0])
            wait_like(frm.at[j, t, 1], s_frm.at[j, t, 1])
            for m, total in enumerate(sums(j, t, ring[t])):
                module = level * choices + m
                total = total + frm[j, t, 0, m].astype(F32) + frm[j, t, 1, m].astype(F32)
                grad = total / jnp.full(total.shape, counts[module], F32)
                new_mom = 0.9 * momb[slot, m, :, lanes_of[t]] + grad
                new = state[module, at, lanes_of[t]] - 0.7 * (grad + 0.9 * new_mom)
                state[module, at, lanes_of[t]] = new
                dense[j, t, 0, m] = new.astype(BF16)
            own = dense.at[j, t, 0]
            p_copy(own.at[first], dense.at[j, t, 3, first], o_bi.at[0], s_bf.at[j, t, 0], ring_up[t])
            p_copy(own.at[second], dense.at[j, t, 1, second], o_bi.at[0], s_bf.at[j, t, 1], ring_down[t])
            p_copy(own.at[second], dense.at[j, t, 3, second], o_bi.at[0], s_bi.at[j, t], ring_up[t])
            p_copy(own.at[first], dense.at[j, t, 1, first], o_bi.at[0], s_bi.at[j, t], ring_down[t])

    def step4(j):
        for t in range(2):
            wait_like(dense.at[j, t, 3, first], s_bf.at[j, t, 0])
            p_copy(dense.at[j, t, 3, first], dense.at[j, t, 2, first], o_bi.at[0], s_bi.at[j, t], ring_up[t])
            wait_like(dense.at[j, t, 1, second], s_bf.at[j, t, 1])
            p_copy(dense.at[j, t, 1, second], dense.at[j, t, 2, second], o_bi.at[0], s_bi.at[j, t], ring_down[t])

    def step5(j):
        level = j // per_level
        at = rows_of(j)
        chunk = lax.rem(j, per_level)
        for t in range(2):
            wait_like(dense.at[j, t, pl.ds(0, 2)], s_bi.at[j, t])
            for k in range(SIDE):
                pick[t, k] = dense[j, t, k]

            @pl.loop(0, group)
            def _(s):
                need = table[level, direct_peer(t, s)]
                for k in range(SIDE):
                    rec[j, t, s, lax.rem(ring[t] + k, SIDE)] = pick[t, k, need]

        def send(dst):
            @pl.loop(1, group)
            def _(i):
                for t in range(2):
                    slot = direct_slot(t, i)
                    p_copy(rec.at[j, t, slot], dst(t), o_b.at[0], s_b.at[j, t], direct_peer(t, slot))

            for t in range(2):
                pltpu.make_async_copy(rec.at[j, t, direct[t] * 2 + core], dst(t), s_b.at[j, t]).start()

        @pl.when(level == 0)
        def _():
            def dst(t):
                if t == 0:
                    return wup.at[y, :, core, at, lanes_of[0]]
                return wup.at[:, x, core, at, lanes_of[1]]

            send(dst)

        @pl.when(level == 1)
        def _():
            def dst(t):
                if t == 0:
                    return wdn.at[chunk, y, :, core, :, lanes_of[0]]
                return wdn.at[chunk, :, x, core, :, lanes_of[1]]

            send(dst)

    top, low = pl.ds(0, half), pl.ds(half, half)
    opposite = lax.rem(z + 2, n_shard)

    def first_projection():
        wait_like(nrm.at[left, low], ag_l.at[1])
        wait_like(nrm.at[right, top], ag_r.at[0])
        wait_like(nrm.at[opposite, top], ag_f.at[0])
        wait_like(nrm.at[opposite, low], ag_f.at[1])
        wait_like(nrm.at[pl.ds(0, 3)], ag_snd.at[0])

        @pl.loop(0, n_shard)
        def _(d):
            value = jnp.dot(
                nrm[lax.rem(z + d, n_shard)], wup[...].reshape(n_path * rows, cols), preferred_element_type=F32
            )
            hid[d] = (value / (1.0 + jnp.exp(-value))).astype(BF16)

    def features(c):
        return pl.ds(pl.multiple_of(c * block, block), block)

    def rs_first(c):
        at = features(c)
        value = lax.dot_general(
            hid[...].reshape(n_shard * tokens, cols),
            wdn[c].reshape(block, cols),
            (((1,), (1,)), ((), ())),
            preferred_element_type=F32,
        ).astype(BF16)
        nrm[:, :, at] = value.reshape(n_shard, tokens, block)
        z_copy(nrm.at[2, top, at], rs_far.at[c, 0], rs_snd.at[0], s_rfar.at[c, 0], right)
        z_copy(nrm.at[2, low, at], rs_far.at[c, 1], rs_snd.at[0], s_rfar.at[c, 1], left)
        z_copy(nrm.at[1, low, at], rs_frm.at[c, 0, low], rs_snd.at[0], s_rfrm.at[c, 0], right)
        z_copy(nrm.at[3, top, at], rs_frm.at[c, 1, top], rs_snd.at[0], s_rfrm.at[c, 1], left)

    def rs_second(c):
        at = features(c)
        wait_like(rs_far.at[c, 0], s_rfar.at[c, 0])
        nrm[1, 0:half, at] = (nrm[1, 0:half, at].astype(F32) + rs_far[c, 0].astype(F32)).astype(BF16)
        z_copy(nrm.at[1, top, at], rs_frm.at[c, 0, top], rs_snd.at[0], s_rfrm.at[c, 0], right)
        wait_like(rs_far.at[c, 1], s_rfar.at[c, 1])
        nrm[3, half:tokens, at] = (nrm[3, half:tokens, at].astype(F32) + rs_far[c, 1].astype(F32)).astype(BF16)
        z_copy(nrm.at[3, low, at], rs_frm.at[c, 1, low], rs_snd.at[0], s_rfrm.at[c, 1], left)

    def rs_last(c):
        wait_like(rs_frm.at[c, 0], s_rfrm.at[c, 0])
        wait_like(rs_frm.at[c, 1], s_rfrm.at[c, 1])
        fit = lax.broadcasted_iota(jnp.int32, (TILE, 128), 1) // TILE == c
        per = 128 // TILE

        @pl.loop(0, tokens // TILE)
        def _(i):
            at = pl.ds(pl.multiple_of(i * TILE, TILE), TILE)
            for g in range(block // 128):
                lanes = pl.ds(g * 128, 128)
                total = (
                    nrm[0, at, pl.ds(pl.multiple_of(c * block + g * 128, 128), 128)].astype(F32)
                    + rs_frm[c, 0, at, lanes].astype(F32)
                    + rs_frm[c, 1, at, lanes].astype(F32)
                )
                for q in range(per):
                    place = pl.ds((g * per + q) * 128, 128)
                    moved = pltpu.roll(total, lax.rem(c + per - q, per) * TILE, 1)
                    old = out[at, place].astype(F32)
                    out[at, place] = jnp.where(fit, old + moved, old).astype(BF16)

    for j in range(AHEAD):
        send_deltas(j)

    @pl.loop(0, levels)
    def _(level):
        for m in range(choices):
            def count(p, total):
                named = jnp.where(table[level, p] == m, 1.0, 0.0)
                wts[(level * n_path + p) * choices + m] = named
                return total + named

            counts[level * choices + m] = lax.fori_loop(0, n_path, count, jnp.float32(0.0))

    load_x.wait()

    @pl.loop(0, tokens // TILE)
    def _(i):
        at = pl.ds(pl.multiple_of(i * TILE, TILE), TILE)
        xf = out[at, :].astype(F32)
        scale = lax.rsqrt(jnp.mean(xf * xf, axis=1, keepdims=True) + 1e-06)
        nrm[z, at, :] = (xf * scale).astype(BF16)

    z_copy(nrm.at[z, top], nrm.at[z, top], ag_snd.at[0], ag_l.at[0], right)
    z_copy(nrm.at[z, low], nrm.at[z, low], ag_snd.at[0], ag_r.at[1], left)
    z_copy(nrm.at[z, low], nrm.at[z, low], ag_snd.at[0], ag_l.at[1], right)
    z_copy(nrm.at[z, top], nrm.at[z, top], ag_snd.at[0], ag_r.at[0], left)
    load_m.wait()

    @pl.loop(0, jobs + 4)
    def _(n):
        def when(low_job, job, high_job, *steps):
            @pl.when((job >= low_job) & (job < high_job))
            def _():
                for step in steps:
                    step()

        when(0, n - 0, jobs, lambda: step1(n - 0))
        when(0, n - 1, jobs, lambda: step3(n - 1))
        when(0, n - 2, jobs, lambda: step5(n - 2))
        when(0, n + AHEAD, jobs, lambda: send_deltas(n + AHEAD))

        def arrived():
            for t in range(2):
                wait_like(rec.at[n - 3, t], s_b.at[n - 3, t])

        when(0, n - 3, jobs, arrived)
        when(per_level - 1, n - 3, per_level, first_projection)
        when(per_level, n - 3, jobs, lambda: rs_first(n - 3 - per_level))
        when(per_level, n - 4, jobs, lambda: rs_last(n - 4 - per_level))
        when(0, n - 0, jobs, lambda: step2(n - 0))
        when(0, n - 1, jobs, lambda: step4(n - 1))
        @pl.when(n == 4)
        def _():
            wait_like(nrm.at[left, top], ag_l.at[0])
            z_copy(nrm.at[left, top], nrm.at[left, top], ag_snd.at[0], ag_f.at[0], right)
            wait_like(nrm.at[right, low], ag_r.at[1])
            z_copy(nrm.at[right, low], nrm.at[right, low], ag_snd.at[0], ag_f.at[1], left)

        when(per_level, n - 3, jobs, lambda: rs_second(n - 3 - per_level))

    others = pl.ds(0, group - 1)
    wait_like(rec.at[:, :, others], o_a.at[0])
    wait_like(rec.at[:, :, others], o_b.at[0])
    wait_like(dense.at[:, :, pl.ds(0, 3)], o_bi.at[0])
    for j in range(jobs - SLOTS, jobs):
        wait_like(part.at[j % SLOTS], o_p.at[j])
    wait_like(nrm.at[pl.ds(0, 3)], rs_snd.at[0])


def per_device(path_table, master, momentum, deltas, activations):
    n_path = lax.axis_size("path")
    n_shard = lax.axis_size("shard")
    levels = deltas.shape[1]
    modules, rows, cols = master.shape
    choices = modules // levels
    tokens, width = activations.shape
    group = n_path // SIDE
    per_level = rows // TILE
    jobs = levels * per_level
    hbm = pl.BlockSpec(memory_space=pl.ANY)
    vmem = pl.BlockSpec(memory_space=pltpu.VMEM)
    smem = pl.BlockSpec(memory_space=pltpu.SMEM)
    dma = pltpu.SemaphoreType.DMA
    block = n_path * TILE
    wide = cols // 2
    return tuple(pl.pallas_call(
        kernel,
        out_shape=(
            pltpu.VMEM((modules, rows, cols), F32),
            pltpu.VMEM((tokens, width), BF16),
        ),
        in_specs=[smem, hbm, hbm, hbm, hbm],
        out_specs=(vmem, vmem),
        scratch_shapes=[
            pltpu.SMEM((levels * n_path * choices,), F32),
            pltpu.SMEM((modules,), F32),
            pltpu.VMEM((n_shard, tokens, width), BF16),
            pltpu.VMEM((SLOTS, choices, TILE, cols), F32),
            pltpu.VMEM((jobs, 2, group, SIDE, TILE, wide), BF16),
            pltpu.VMEM((SLOTS, 2, 3, choices, TILE, wide), BF16),
            pltpu.VMEM((jobs, 2, 2, choices // 2, TILE, wide), BF16),
            pltpu.VMEM((jobs, 2, 2, choices, TILE, wide), BF16),
            pltpu.VMEM((jobs, 2, SIDE, choices, TILE, wide), BF16),
            pltpu.VMEM((2, SIDE, choices, TILE, wide), BF16),
            pltpu.VMEM((SIDE, SIDE, 2, rows, cols), BF16),
            pltpu.VMEM((per_level, SIDE, SIDE, 2, TILE, cols), BF16),
            pltpu.VMEM((n_shard, tokens, cols), BF16),
            pltpu.VMEM((per_level, 2, tokens // 2, block), BF16),
            pltpu.VMEM((per_level, 2, tokens, block), BF16),
            dma((jobs, 2)), dma((jobs, 2, 2)), dma((jobs, 2, 2)), dma((jobs, 2)), dma((jobs, 2, 2)), dma((jobs, 2)),
            dma((1,)), dma((jobs,)), dma((1,)), dma((1,)),
            dma((1,)), dma((2,)), dma((2,)), dma((2,)),
            dma((1,)), dma((per_level, 2)), dma((per_level, 2)),
            dma((2,)), dma((SLOTS,)),
        ],
        compiler_params=pltpu.CompilerParams(
            collective_id=0, has_side_effects=True, vmem_limit_bytes=56 * 1024 * 1024
        ),
    )(
        path_table.T,
        master,
        momentum,
        deltas.reshape(levels, SIDE, SIDE, 2, rows, cols),
        activations,
    ))


def solution(mesh):
    placed = (
        P(),
        P(None, "path", "shard"),
        P(None, "path", "shard"),
        P("path", None, None, "shard"),
        P(("path", "shard"), None),
    )
    return jax.shard_map(
        per_device,
        mesh=mesh,
        in_specs=placed,
        out_specs=(P(None, "path", "shard"), P(("path", "shard"), None)),
        check_vma=False,
    )
```

```python
import jax
import jax.numpy as jnp
from jax import lax
from jax.experimental import pallas as pl
from jax.experimental.pallas import tpu as pltpu
from jax.sharding import PartitionSpec as P

MESH = pl.DeviceIdType.MESH
F32 = jnp.float32
BF16 = jnp.bfloat16

TILE = 16
SLOTS = 4
AHEAD = 2
SIDE = 4


def kernel(
    table, master, momentum, deltas, acts,
    state, out,
    wts, counts,
    nrm, momb, rec, part, far, frm, dense, pick, wup, wdn, hid, rs_far, rs_frm,
    s_a, s_far, s_frm, s_bi, s_bf, s_b,
    o_a, o_p, o_bi, o_b,
    ag_snd, ag_l, ag_r, ag_f,
    rs_snd, s_rfar, s_rfrm,
    sem_in, sem_mom,
):
    levels = deltas.shape[0]
    rows = deltas.shape[4]
    cols = deltas.shape[5]
    jobs = rec.shape[0]
    per_level = jobs // levels
    choices = dense.shape[3]
    group = rec.shape[2]
    n_path = SIDE * group
    n_shard, tokens, width = nrm.shape
    half = tokens // 2
    some = choices // 2
    lanes_of = [pl.ds(t * (cols // 2), cols // 2) for t in range(2)]
    block = n_path * TILE

    me = lax.axis_index("path")
    z = lax.axis_index("shard")
    core = lax.rem(me, 2)
    x = lax.rem(me // 2, SIDE)
    y = me // group
    right = lax.rem(z + 1, n_shard)
    left = lax.rem(z + n_shard - 1, n_shard)
    direct = (y, x)
    ring = (x, y)

    def path_of(t, d, r, c):
        return (d * SIDE + r) * 2 + c if t == 0 else (r * SIDE + d) * 2 + c

    def member(t, s):
        return path_of(t, s // 2, ring[t], s % 2)

    def offset(i):
        return lax.rem(i * 3, group)

    def direct_slot(t, i):
        j = offset(i)
        return lax.rem(direct[t] + j // 2, SIDE) * 2 + lax.rem(core + j, 2)

    def direct_peer(t, slot):
        return path_of(t, slot // 2, ring[t], lax.rem(slot, 2))

    ring_up = [path_of(t, direct[t], lax.rem(ring[t] + 1, SIDE), core) for t in range(2)]
    ring_down = [path_of(t, direct[t], lax.rem(ring[t] + SIDE - 1, SIDE), core) for t in range(2)]

    load_x = pltpu.make_async_copy(acts, out, sem_in.at[0])
    load_x.start()
    load_m = pltpu.make_async_copy(master, state, sem_in.at[1])
    load_m.start()

    barrier = pltpu.get_barrier_semaphore()

    @pl.loop(1, group)
    def _(i):
        slot = direct_slot(0, i)
        pl.semaphore_signal(barrier, inc=1, device_id={"path": direct_peer(0, slot)}, device_id_type=MESH)

    @pl.loop(2, group)
    def _(i):
        slot = lax.rem(direct[1] + i // 2, SIDE) * 2 + lax.rem(core + i, 2)
        pl.semaphore_signal(barrier, inc=1, device_id={"path": direct_peer(1, slot)}, device_id_type=MESH)

    for side in (left, right):
        pl.semaphore_signal(barrier, inc=1, device_id={"shard": side}, device_id_type=MESH)
    pl.semaphore_wait(barrier, (group - 1) + (group - 2) + 2)

    def wait_like(ref, sem):
        pltpu.make_async_copy(ref, ref, sem).wait()

    def p_copy(src, dst, send, recv, peer):
        pltpu.make_async_remote_copy(
            src, dst, send, recv, device_id={"path": peer}, device_id_type=MESH
        ).start()

    def z_copy(src, dst, send, recv, side):
        pltpu.make_async_remote_copy(
            src, dst, send, recv, device_id={"shard": side}, device_id_type=MESH
        ).start()

    def rows_of(j):
        return pl.ds(pl.multiple_of(lax.rem(j, per_level) * TILE, TILE), TILE)

    def send_deltas(j):
        level = j // per_level
        at = rows_of(j)

        def src(t, slot):
            d, c = slot // 2, lax.rem(slot, 2)
            if t == 0:
                return deltas.at[level, d, :, c, at, lanes_of[0]]
            return deltas.at[level, :, d, c, at, lanes_of[1]]

        def dst(t):
            return rec.at[j, t, direct[t] * 2 + core]

        @pl.loop(1, group)
        def _(i):
            for t in range(2):
                slot = direct_slot(t, i)
                p_copy(src(t, slot), dst(t), o_a.at[0], s_a.at[j, t], direct_peer(t, slot))

        for t in range(2):
            pltpu.make_async_copy(src(t, direct[t] * 2 + core), dst(t), s_a.at[j, t]).start()

    def sums(j, t, owner):
        base = (j // per_level) * n_path
        total = [None] * choices
        for s in range(group):
            value = rec[j, t, s, owner].astype(F32)
            at = (base + member(t, s)) * choices
            for m in range(choices):
                term = wts[at + m] * value
                total[m] = term if total[m] is None else total[m] + term
        return total

    def momentum_copy(j):
        level = j // per_level
        slot = lax.rem(j, SLOTS)
        return pltpu.make_async_copy(
            momentum.at[pl.ds(level * choices, choices), rows_of(j)], momb.at[slot], sem_mom.at[slot]
        )

    first, second = pl.ds(0, some), pl.ds(some, some)

    def step1(j):
        slot = lax.rem(j, SLOTS)

        @pl.when(j >= SLOTS)
        def _():
            wait_like(part.at[slot], o_p.at[j - SLOTS])

        momentum_copy(j).start()
        for t in range(2):
            wait_like(rec.at[j, t], s_a.at[j, t])

        def fill(t, k):
            for m, value in enumerate(sums(j, t, lax.rem(ring[t] + k, SIDE))):
                part[slot, t, k - 1, m] = value.astype(BF16)

        for t in range(2):
            fill(t, 2)
            p_copy(part.at[slot, t, 1, first], far.at[j, t, 0], o_p.at[j], s_far.at[j, t, 0], ring_up[t])
            p_copy(part.at[slot, t, 1, second], far.at[j, t, 1], o_p.at[j], s_far.at[j, t, 1], ring_down[t])
        for t in range(2):
            fill(t, 1)
            p_copy(part.at[slot, t, 0, second], frm.at[j, t, 0, second], o_p.at[j], s_frm.at[j, t, 0], ring_up[t])
            fill(t, 3)
            p_copy(part.at[slot, t, 2, first], frm.at[j, t, 1, first], o_p.at[j], s_frm.at[j, t, 1], ring_down[t])

    def step2(j):
        slot = lax.rem(j, SLOTS)
        for t in range(2):
            wait_like(far.at[j, t, 0], s_far.at[j, t, 0])
            for m in range(some):
                part[slot, t, 0, m] = (part[slot, t, 0, m].astype(F32) + far[j, t, 0, m].astype(F32)).astype(BF16)
            p_copy(part.at[slot, t, 0, first], frm.at[j, t, 0, first], o_p.at[j], s_frm.at[j, t, 0], ring_up[t])
            wait_like(far.at[j, t, 1], s_far.at[j, t, 1])
            for m in range(some):
                n = some + m
                part[slot, t, 2, n] = (part[slot, t, 2, n].astype(F32) + far[j, t, 1, m].astype(F32)).astype(BF16)
            p_copy(part.at[slot, t, 2, second], frm.at[j, t, 1, second], o_p.at[j], s_frm.at[j, t, 1], ring_down[t])

    def step3(j):
        level = j // per_level
        slot = lax.rem(j, SLOTS)
        at = rows_of(j)
        momentum_copy(j).wait()
        for t in range(2):
            wait_like(frm.at[j, t, 0], s_frm.at[j, t, 0])
            wait_like(frm.at[j, t, 1], s_frm.at[j, t, 1])
            for m, total in enumerate(sums(j, t, ring[t])):
                module = level * choices + m
                total = total + frm[j, t, 0, m].astype(F32) + frm[j, t, 1, m].astype(F32)
                grad = total / jnp.full(total.shape, counts[module], F32)
                new_mom = 0.9 * momb[slot, m, :, lanes_of[t]] + grad
                new = state[module, at, lanes_of[t]] - 0.7 * (grad + 0.9 * new_mom)
                state[module, at, lanes_of[t]] = new
                dense[j, t, 0, m] = new.astype(BF16)
            own = dense.at[j, t, 0]
            p_copy(own.at[first], dense.at[j, t, 3, first], o_bi.at[0], s_bf.at[j, t, 0], ring_up[t])
            p_copy(own.at[second], dense.at[j, t, 1, second], o_bi.at[0], s_bf.at[j, t, 1], ring_down[t])
            p_copy(own.at[second], dense.at[j, t, 3, second], o_bi.at[0], s_bi.at[j, t], ring_up[t])
            p_copy(own.at[first], dense.at[j, t, 1, first], o_bi.at[0], s_bi.at[j, t], ring_down[t])

    def step4(j):
        for t in range(2):
            wait_like(dense.at[j, t, 3, first], s_bf.at[j, t, 0])
            p_copy(dense.at[j, t, 3, first], dense.at[j, t, 2, first], o_bi.at[0], s_bi.at[j, t], ring_up[t])
            wait_like(dense.at[j, t, 1, second], s_bf.at[j, t, 1])
            p_copy(dense.at[j, t, 1, second], dense.at[j, t, 2, second], o_bi.at[0], s_bi.at[j, t], ring_down[t])

    def step5(j):
        level = j // per_level
        at = rows_of(j)
        chunk = lax.rem(j, per_level)
        for t in range(2):
            wait_like(dense.at[j, t, pl.ds(0, 2)], s_bi.at[j, t])
            for k in range(SIDE):
                pick[t, k] = dense[j, t, k]

            @pl.loop(0, group)
            def _(s):
                need = table[level, direct_peer(t, s)]
                for k in range(SIDE):
                    rec[j, t, s, lax.rem(ring[t] + k, SIDE)] = pick[t, k, need]

        def send(dst):
            @pl.loop(1, group)
            def _(i):
                for t in range(2):
                    slot = direct_slot(t, i)
                    p_copy(rec.at[j, t, slot], dst(t), o_b.at[0], s_b.at[j, t], direct_peer(t, slot))

            for t in range(2):
                pltpu.make_async_copy(rec.at[j, t, direct[t] * 2 + core], dst(t), s_b.at[j, t]).start()

        @pl.when(level == 0)
        def _():
            def dst(t):
                if t == 0:
                    return wup.at[y, :, core, at, lanes_of[0]]
                return wup.at[:, x, core, at, lanes_of[1]]

            send(dst)

        @pl.when(level == 1)
        def _():
            def dst(t):
                if t == 0:
                    return wdn.at[chunk, y, :, core, :, lanes_of[0]]
                return wdn.at[chunk, :, x, core, :, lanes_of[1]]

            send(dst)

    top, low = pl.ds(0, half), pl.ds(half, half)
    opposite = lax.rem(z + 2, n_shard)

    def first_projection():
        wait_like(nrm.at[left, low], ag_l.at[1])
        wait_like(nrm.at[right, top], ag_r.at[0])
        wait_like(nrm.at[opposite, top], ag_f.at[0])
        wait_like(nrm.at[opposite, low], ag_f.at[1])
        wait_like(nrm.at[pl.ds(0, 3)], ag_snd.at[0])

        @pl.loop(0, n_shard)
        def _(d):
            value = jnp.dot(
                nrm[lax.rem(z + 2 + 3 * d, n_shard)], wup[...].reshape(n_path * rows, cols), preferred_element_type=F32
            )
            hid[d] = (value / (1.0 + jnp.exp(-value))).astype(BF16)

    def features(c):
        return pl.ds(pl.multiple_of(c * block, block), block)

    def rs_first(c):
        at = features(c)

        def product(first_block, count):
            value = lax.dot_general(
                hid[first_block:first_block + count].reshape(count * tokens, cols),
                wdn[c].reshape(block, cols),
                (((1,), (1,)), ((), ())),
                preferred_element_type=F32,
            ).astype(BF16)
            nrm[first_block:first_block + count, :, at] = value.reshape(count, tokens, block)

        product(0, 1)
        z_copy(nrm.at[0, top, at], rs_far.at[c, 0], rs_snd.at[0], s_rfar.at[c, 0], right)
        z_copy(nrm.at[0, low, at], rs_far.at[c, 1], rs_snd.at[0], s_rfar.at[c, 1], left)
        product(1, 3)
        z_copy(nrm.at[1, low, at], rs_frm.at[c, 0, low], rs_snd.at[0], s_rfrm.at[c, 0], right)
        z_copy(nrm.at[3, top, at], rs_frm.at[c, 1, top], rs_snd.at[0], s_rfrm.at[c, 1], left)

    def rs_second(c):
        at = features(c)
        wait_like(rs_far.at[c, 0], s_rfar.at[c, 0])
        nrm[1, 0:half, at] = (nrm[1, 0:half, at].astype(F32) + rs_far[c, 0].astype(F32)).astype(BF16)
        z_copy(nrm.at[1, top, at], rs_frm.at[c, 0, top], rs_snd.at[0], s_rfrm.at[c, 0], right)
        wait_like(rs_far.at[c, 1], s_rfar.at[c, 1])
        nrm[3, half:tokens, at] = (nrm[3, half:tokens, at].astype(F32) + rs_far[c, 1].astype(F32)).astype(BF16)
        z_copy(nrm.at[3, low, at], rs_frm.at[c, 1, low], rs_snd.at[0], s_rfrm.at[c, 1], left)

    def rs_last(c):
        wait_like(rs_frm.at[c, 0], s_rfrm.at[c, 0])
        wait_like(rs_frm.at[c, 1], s_rfrm.at[c, 1])
        fit = lax.broadcasted_iota(jnp.int32, (TILE, 128), 1) // TILE == c
        per = 128 // TILE

        @pl.loop(0, tokens // TILE)
        def _(i):
            at = pl.ds(pl.multiple_of(i * TILE, TILE), TILE)
            for g in range(block // 128):
                lanes = pl.ds(g * 128, 128)
                total = (
                    nrm[2, at, pl.ds(pl.multiple_of(c * block + g * 128, 128), 128)].astype(F32)
                    + rs_frm[c, 0, at, lanes].astype(F32)
                    + rs_frm[c, 1, at, lanes].astype(F32)
                )
                places = [pl.ds((g * per + q) * 128, 128) for q in range(per)]
                olds = [out[at, place].astype(F32) for place in places]
                moved = [pltpu.roll(total, lax.rem(c + per - q, per) * TILE, 1) for q in range(per)]
                for q in range(per):
                    out[at, places[q]] = jnp.where(fit, olds[q] + moved[q], olds[q]).astype(BF16)

    for j in range(AHEAD):
        send_deltas(j)

    @pl.loop(0, levels)
    def _(level):
        for m in range(choices):
            def count(p, total):
                named = jnp.where(table[level, p] == m, 1.0, 0.0)
                wts[(level * n_path + p) * choices + m] = named
                return total + named

            counts[level * choices + m] = lax.fori_loop(0, n_path, count, jnp.float32(0.0))

    load_x.wait()

    @pl.loop(0, tokens // TILE)
    def _(i):
        at = pl.ds(pl.multiple_of(i * TILE, TILE), TILE)
        xf = out[at, :].astype(F32)
        scale = lax.rsqrt(jnp.mean(xf * xf, axis=1, keepdims=True) + 1e-06)
        nrm[z, at, :] = (xf * scale).astype(BF16)

    z_copy(nrm.at[z, top], nrm.at[z, top], ag_snd.at[0], ag_l.at[0], right)
    z_copy(nrm.at[z, low], nrm.at[z, low], ag_snd.at[0], ag_r.at[1], left)
    z_copy(nrm.at[z, low], nrm.at[z, low], ag_snd.at[0], ag_l.at[1], right)
    z_copy(nrm.at[z, top], nrm.at[z, top], ag_snd.at[0], ag_r.at[0], left)
    load_m.wait()

    @pl.loop(0, jobs + 5)
    def _(n):
        def when(low_job, job, high_job, *steps):
            @pl.when((job >= low_job) & (job < high_job))
            def _():
                for step in steps:
                    step()

        when(0, n - 2, jobs, lambda: step3(n - 2))

        def arrived():
            for t in range(2):
                wait_like(rec.at[n - 4, t], s_b.at[n - 4, t])

        when(0, n - 4, jobs, arrived)
        when(per_level, n - 4, jobs, lambda: rs_first(n - 4 - per_level))
        when(0, n - 1, jobs, lambda: step2(n - 1))
        when(0, n - 3, jobs, lambda: step5(n - 3))
        when(0, n, jobs, lambda: step1(n))
        @pl.when(n == 4)
        def _():
            wait_like(nrm.at[left, top], ag_l.at[0])
            z_copy(nrm.at[left, top], nrm.at[left, top], ag_snd.at[0], ag_f.at[0], right)
            wait_like(nrm.at[right, low], ag_r.at[1])
            z_copy(nrm.at[right, low], nrm.at[right, low], ag_snd.at[0], ag_f.at[1], left)

        when(per_level, n - 5, jobs, lambda: rs_last(n - 5 - per_level))
        when(per_level, n - 4, jobs, lambda: rs_second(n - 4 - per_level))
        when(per_level - 1, n - 4, per_level, first_projection)
        when(0, n - 2, jobs, lambda: step4(n - 2))
        when(0, n + AHEAD, jobs, lambda: send_deltas(n + AHEAD))

    others = pl.ds(0, group - 1)
    wait_like(rec.at[:, :, others], o_a.at[0])
    wait_like(rec.at[:, :, others], o_b.at[0])
    wait_like(dense.at[:, :, pl.ds(0, 3)], o_bi.at[0])
    for j in range(jobs - SLOTS, jobs):
        wait_like(part.at[j % SLOTS], o_p.at[j])
    wait_like(nrm.at[pl.ds(0, 3)], rs_snd.at[0])


def per_device(path_table, master, momentum, deltas, activations):
    n_path = lax.axis_size("path")
    n_shard = lax.axis_size("shard")
    levels = deltas.shape[1]
    modules, rows, cols = master.shape
    choices = modules // levels
    tokens, width = activations.shape
    group = n_path // SIDE
    per_level = rows // TILE
    jobs = levels * per_level
    hbm = pl.BlockSpec(memory_space=pl.ANY)
    vmem = pl.BlockSpec(memory_space=pltpu.VMEM)
    smem = pl.BlockSpec(memory_space=pltpu.SMEM)
    dma = pltpu.SemaphoreType.DMA
    block = n_path * TILE
    wide = cols // 2
    return tuple(pl.pallas_call(
        kernel,
        out_shape=(
            pltpu.VMEM((modules, rows, cols), F32),
            pltpu.VMEM((tokens, width), BF16),
        ),
        in_specs=[smem, hbm, hbm, hbm, hbm],
        out_specs=(vmem, vmem),
        scratch_shapes=[
            pltpu.SMEM((levels * n_path * choices,), F32),
            pltpu.SMEM((modules,), F32),
            pltpu.VMEM((n_shard, tokens, width), BF16),
            pltpu.VMEM((SLOTS, choices, TILE, cols), F32),
            pltpu.VMEM((jobs, 2, group, SIDE, TILE, wide), BF16),
            pltpu.VMEM((SLOTS, 2, 3, choices, TILE, wide), BF16),
            pltpu.VMEM((jobs, 2, 2, choices // 2, TILE, wide), BF16),
            pltpu.VMEM((jobs, 2, 2, choices, TILE, wide), BF16),
            pltpu.VMEM((jobs, 2, SIDE, choices, TILE, wide), BF16),
            pltpu.VMEM((2, SIDE, choices, TILE, wide), BF16),
            pltpu.VMEM((SIDE, SIDE, 2, rows, cols), BF16),
            pltpu.VMEM((per_level, SIDE, SIDE, 2, TILE, cols), BF16),
            pltpu.VMEM((n_shard, tokens, cols), BF16),
            pltpu.VMEM((per_level, 2, tokens // 2, block), BF16),
            pltpu.VMEM((per_level, 2, tokens, block), BF16),
            dma((jobs, 2)), dma((jobs, 2, 2)), dma((jobs, 2, 2)), dma((jobs, 2)), dma((jobs, 2, 2)), dma((jobs, 2)),
            dma((1,)), dma((jobs,)), dma((1,)), dma((1,)),
            dma((1,)), dma((2,)), dma((2,)), dma((2,)),
            dma((1,)), dma((per_level, 2)), dma((per_level, 2)),
            dma((2,)), dma((SLOTS,)),
        ],
        compiler_params=pltpu.CompilerParams(
            collective_id=0, has_side_effects=True, vmem_limit_bytes=56 * 1024 * 1024
        ),
    )(
        path_table.T,
        master,
        momentum,
        deltas.reshape(levels, SIDE, SIDE, 2, rows, cols),
        activations,
    ))


def solution(mesh):
    placed = (
        P(),
        P(None, "path", "shard"),
        P(None, "path", "shard"),
        P("path", None, None, "shard"),
        P(("path", "shard"), None),
    )
    return jax.shard_map(
        per_device,
        mesh=mesh,
        in_specs=placed,
        out_specs=(P(None, "path", "shard"), P(("path", "shard"), None)),
        check_vma=False,
    )
```

```python
import jax
import jax.numpy as jnp
from jax import lax
from jax.experimental import pallas as pl
from jax.experimental.pallas import tpu as pltpu
from jax.sharding import PartitionSpec as P

MESH = pl.DeviceIdType.MESH
F32 = jnp.float32
BF16 = jnp.bfloat16

TILE = 16
SLOTS = 4
AHEAD = 2
SIDE = 4


def kernel(
    table, master, momentum, deltas, acts,
    state, out,
    wts, counts,
    nrm, momb, rec, part, far, frm, dense, pick, wup, wdn, hid, rs_far, rs_frm,
    s_a, s_far, s_frm, s_bi, s_bf, s_b,
    o_a, o_p, o_bi, o_b,
    ag_snd, ag_l, ag_r, ag_f,
    rs_snd, s_rfar, s_rfrm,
    sem_in, sem_mom,
):
    levels = deltas.shape[0]
    rows = deltas.shape[4]
    cols = deltas.shape[5]
    jobs = rec.shape[0]
    per_level = jobs // levels
    choices = dense.shape[3]
    group = rec.shape[2]
    n_path = SIDE * group
    n_shard, tokens, width = nrm.shape
    half = tokens // 2
    some = choices // 2
    lanes_of = [pl.ds(t * (cols // 2), cols // 2) for t in range(2)]
    block = n_path * TILE

    me = lax.axis_index("path")
    z = lax.axis_index("shard")
    core = lax.rem(me, 2)
    x = lax.rem(me // 2, SIDE)
    y = me // group
    right = lax.rem(z + 1, n_shard)
    left = lax.rem(z + n_shard - 1, n_shard)
    direct = (y, x)
    ring = (x, y)

    def path_of(t, d, r, c):
        return (d * SIDE + r) * 2 + c if t == 0 else (r * SIDE + d) * 2 + c

    def member(t, s):
        return path_of(t, s // 2, ring[t], s % 2)

    def offset(i):
        return lax.rem(i * 3, group)

    def direct_slot(t, i):
        j = offset(i)
        return lax.rem(direct[t] + j // 2, SIDE) * 2 + lax.rem(core + j, 2)

    def direct_peer(t, slot):
        return path_of(t, slot // 2, ring[t], lax.rem(slot, 2))

    ring_up = [path_of(t, direct[t], lax.rem(ring[t] + 1, SIDE), core) for t in range(2)]
    ring_down = [path_of(t, direct[t], lax.rem(ring[t] + SIDE - 1, SIDE), core) for t in range(2)]

    load_x = pltpu.make_async_copy(acts, out, sem_in.at[0])
    load_x.start()
    load_m = pltpu.make_async_copy(master, state, sem_in.at[1])
    load_m.start()

    barrier = pltpu.get_barrier_semaphore()

    @pl.loop(1, group)
    def _(i):
        slot = direct_slot(0, i)
        pl.semaphore_signal(barrier, inc=1, device_id={"path": direct_peer(0, slot)}, device_id_type=MESH)

    @pl.loop(2, group)
    def _(i):
        slot = lax.rem(direct[1] + i // 2, SIDE) * 2 + lax.rem(core + i, 2)
        pl.semaphore_signal(barrier, inc=1, device_id={"path": direct_peer(1, slot)}, device_id_type=MESH)

    for side in (left, right):
        pl.semaphore_signal(barrier, inc=1, device_id={"shard": side}, device_id_type=MESH)
    pl.semaphore_wait(barrier, (group - 1) + (group - 2) + 2)

    def wait_like(ref, sem):
        pltpu.make_async_copy(ref, ref, sem).wait()

    def p_copy(src, dst, send, recv, peer):
        pltpu.make_async_remote_copy(
            src, dst, send, recv, device_id={"path": peer}, device_id_type=MESH
        ).start()

    def z_copy(src, dst, send, recv, side):
        pltpu.make_async_remote_copy(
            src, dst, send, recv, device_id={"shard": side}, device_id_type=MESH
        ).start()

    def rows_of(j):
        return pl.ds(pl.multiple_of(lax.rem(j, per_level) * TILE, TILE), TILE)

    def send_deltas(j):
        level = j // per_level
        at = rows_of(j)

        def src(t, slot):
            d, c = slot // 2, lax.rem(slot, 2)
            if t == 0:
                return deltas.at[level, d, :, c, at, lanes_of[0]]
            return deltas.at[level, :, d, c, at, lanes_of[1]]

        def dst(t):
            return rec.at[j, t, direct[t] * 2 + core]

        @pl.loop(1, group)
        def _(i):
            for t in range(2):
                slot = direct_slot(t, i)
                p_copy(src(t, slot), dst(t), o_a.at[0], s_a.at[j, t], direct_peer(t, slot))

        for t in range(2):
            pltpu.make_async_copy(src(t, direct[t] * 2 + core), dst(t), s_a.at[j, t]).start()

    def sums(j, t, owner):
        base = (j // per_level) * n_path
        total = [None] * choices
        for s in range(group):
            value = rec[j, t, s, owner].astype(F32)
            at = (base + member(t, s)) * choices
            for m in range(choices):
                term = wts[at + m] * value
                total[m] = term if total[m] is None else total[m] + term
        return total

    def momentum_copy(j):
        level = j // per_level
        slot = lax.rem(j, SLOTS)
        return pltpu.make_async_copy(
            momentum.at[pl.ds(level * choices, choices), rows_of(j)], momb.at[slot], sem_mom.at[slot]
        )

    first, second = pl.ds(0, some), pl.ds(some, some)

    def step1(j):
        slot = lax.rem(j, SLOTS)

        @pl.when(j >= SLOTS)
        def _():
            wait_like(part.at[slot], o_p.at[j - SLOTS])

        momentum_copy(j).start()
        for t in range(2):
            wait_like(rec.at[j, t], s_a.at[j, t])

        def fill(t, k):
            for m, value in enumerate(sums(j, t, lax.rem(ring[t] + k, SIDE))):
                part[slot, t, k - 1, m] = value.astype(BF16)

        for t in range(2):
            fill(t, 2)
            p_copy(part.at[slot, t, 1, first], far.at[j, t, 0], o_p.at[j], s_far.at[j, t, 0], ring_up[t])
            p_copy(part.at[slot, t, 1, second], far.at[j, t, 1], o_p.at[j], s_far.at[j, t, 1], ring_down[t])
        for t in range(2):
            fill(t, 1)
            p_copy(part.at[slot, t, 0, second], frm.at[j, t, 0, second], o_p.at[j], s_frm.at[j, t, 0], ring_up[t])
            fill(t, 3)
            p_copy(part.at[slot, t, 2, first], frm.at[j, t, 1, first], o_p.at[j], s_frm.at[j, t, 1], ring_down[t])

    def step2(j):
        slot = lax.rem(j, SLOTS)
        for t in range(2):
            wait_like(far.at[j, t, 0], s_far.at[j, t, 0])
            for m in range(some):
                part[slot, t, 0, m] = (part[slot, t, 0, m].astype(F32) + far[j, t, 0, m].astype(F32)).astype(BF16)
            p_copy(part.at[slot, t, 0, first], frm.at[j, t, 0, first], o_p.at[j], s_frm.at[j, t, 0], ring_up[t])
            wait_like(far.at[j, t, 1], s_far.at[j, t, 1])
            for m in range(some):
                n = some + m
                part[slot, t, 2, n] = (part[slot, t, 2, n].astype(F32) + far[j, t, 1, m].astype(F32)).astype(BF16)
            p_copy(part.at[slot, t, 2, second], frm.at[j, t, 1, second], o_p.at[j], s_frm.at[j, t, 1], ring_down[t])

    def step3(j):
        level = j // per_level
        slot = lax.rem(j, SLOTS)
        at = rows_of(j)
        momentum_copy(j).wait()
        for t in range(2):
            wait_like(frm.at[j, t, 0], s_frm.at[j, t, 0])
            wait_like(frm.at[j, t, 1], s_frm.at[j, t, 1])
            for m, total in enumerate(sums(j, t, ring[t])):
                module = level * choices + m
                total = total + frm[j, t, 0, m].astype(F32) + frm[j, t, 1, m].astype(F32)
                grad = total / jnp.full(total.shape, counts[module], F32)
                new_mom = 0.9 * momb[slot, m, :, lanes_of[t]] + grad
                new = state[module, at, lanes_of[t]] - 0.7 * (grad + 0.9 * new_mom)
                state[module, at, lanes_of[t]] = new
                dense[j, t, 0, m] = new.astype(BF16)
            own = dense.at[j, t, 0]
            p_copy(own.at[first], dense.at[j, t, 3, first], o_bi.at[0], s_bf.at[j, t, 0], ring_up[t])
            p_copy(own.at[second], dense.at[j, t, 1, second], o_bi.at[0], s_bf.at[j, t, 1], ring_down[t])
            p_copy(own.at[second], dense.at[j, t, 3, second], o_bi.at[0], s_bi.at[j, t], ring_up[t])
            p_copy(own.at[first], dense.at[j, t, 1, first], o_bi.at[0], s_bi.at[j, t], ring_down[t])

    def step4(j):
        for t in range(2):
            wait_like(dense.at[j, t, 3, first], s_bf.at[j, t, 0])
            p_copy(dense.at[j, t, 3, first], dense.at[j, t, 2, first], o_bi.at[0], s_bi.at[j, t], ring_up[t])
            wait_like(dense.at[j, t, 1, second], s_bf.at[j, t, 1])
            p_copy(dense.at[j, t, 1, second], dense.at[j, t, 2, second], o_bi.at[0], s_bi.at[j, t], ring_down[t])

    def step5(j):
        level = j // per_level
        at = rows_of(j)
        chunk = lax.rem(j, per_level)
        for t in range(2):
            wait_like(dense.at[j, t, pl.ds(0, 2)], s_bi.at[j, t])
            for k in range(SIDE):
                pick[t, k] = dense[j, t, k]

            @pl.loop(0, group)
            def _(s):
                need = table[level, direct_peer(t, s)]
                for k in range(SIDE):
                    rec[j, t, s, lax.rem(ring[t] + k, SIDE)] = pick[t, k, need]

        def send(dst):
            @pl.loop(1, group)
            def _(i):
                for t in range(2):
                    slot = direct_slot(t, i)
                    p_copy(rec.at[j, t, slot], dst(t), o_b.at[0], s_b.at[j, t], direct_peer(t, slot))

            for t in range(2):
                pltpu.make_async_copy(rec.at[j, t, direct[t] * 2 + core], dst(t), s_b.at[j, t]).start()

        @pl.when(level == 0)
        def _():
            def dst(t):
                if t == 0:
                    return wup.at[y, :, core, at, lanes_of[0]]
                return wup.at[:, x, core, at, lanes_of[1]]

            send(dst)

        @pl.when(level == 1)
        def _():
            def dst(t):
                if t == 0:
                    return wdn.at[chunk, y, :, core, :, lanes_of[0]]
                return wdn.at[chunk, :, x, core, :, lanes_of[1]]

            send(dst)

    top, low = pl.ds(0, half), pl.ds(half, half)
    opposite = lax.rem(z + 2, n_shard)

    def first_projection():
        wait_like(nrm.at[left, low], ag_l.at[1])
        wait_like(nrm.at[right, top], ag_r.at[0])
        wait_like(nrm.at[opposite, top], ag_f.at[0])
        wait_like(nrm.at[opposite, low], ag_f.at[1])
        wait_like(nrm.at[pl.ds(0, 3)], ag_snd.at[0])

        @pl.loop(0, n_shard)
        def _(d):
            value = jnp.dot(
                nrm[lax.rem(z + 2 + 3 * d, n_shard)], wup[...].reshape(n_path * rows, cols), preferred_element_type=F32
            )
            hid[d] = (value / (1.0 + jnp.exp(-value))).astype(BF16)

    def features(c):
        return pl.ds(pl.multiple_of(c * block, block), block)

    def rs_first(c):
        at = features(c)

        def product(first_block, count):
            value = lax.dot_general(
                hid[first_block:first_block + count].reshape(count * tokens, cols),
                wdn[c].reshape(block, cols),
                (((1,), (1,)), ((), ())),
                preferred_element_type=F32,
            ).astype(BF16)
            nrm[first_block:first_block + count, :, at] = value.reshape(count, tokens, block)

        product(0, 1)
        z_copy(nrm.at[0, top, at], rs_far.at[c, 0], rs_snd.at[0], s_rfar.at[c, 0], right)
        z_copy(nrm.at[0, low, at], rs_far.at[c, 1], rs_snd.at[0], s_rfar.at[c, 1], left)
        product(1, 3)
        z_copy(nrm.at[1, low, at], rs_frm.at[c, 0, low], rs_snd.at[0], s_rfrm.at[c, 0], right)
        z_copy(nrm.at[3, top, at], rs_frm.at[c, 1, top], rs_snd.at[0], s_rfrm.at[c, 1], left)

    def rs_second(c):
        at = features(c)
        wait_like(rs_far.at[c, 0], s_rfar.at[c, 0])
        nrm[1, 0:half, at] = (nrm[1, 0:half, at].astype(F32) + rs_far[c, 0].astype(F32)).astype(BF16)
        z_copy(nrm.at[1, top, at], rs_frm.at[c, 0, top], rs_snd.at[0], s_rfrm.at[c, 0], right)
        wait_like(rs_far.at[c, 1], s_rfar.at[c, 1])
        nrm[3, half:tokens, at] = (nrm[3, half:tokens, at].astype(F32) + rs_far[c, 1].astype(F32)).astype(BF16)
        z_copy(nrm.at[3, low, at], rs_frm.at[c, 1, low], rs_snd.at[0], s_rfrm.at[c, 1], left)

    def rs_last(c):
        wait_like(rs_frm.at[c, 0], s_rfrm.at[c, 0])
        wait_like(rs_frm.at[c, 1], s_rfrm.at[c, 1])
        fit = lax.broadcasted_iota(jnp.int32, (TILE, 128), 1) // TILE == c
        per = 128 // TILE

        @pl.loop(0, tokens // TILE)
        def _(i):
            at = pl.ds(pl.multiple_of(i * TILE, TILE), TILE)
            for g in range(block // 128):
                lanes = pl.ds(g * 128, 128)
                total = (
                    nrm[2, at, pl.ds(pl.multiple_of(c * block + g * 128, 128), 128)].astype(F32)
                    + rs_frm[c, 0, at, lanes].astype(F32)
                    + rs_frm[c, 1, at, lanes].astype(F32)
                )
                places = [pl.ds((g * per + q) * 128, 128) for q in range(per)]
                olds = [out[at, place].astype(F32) for place in places]
                moved = [pltpu.roll(total, lax.rem(c + per - q, per) * TILE, 1) for q in range(per)]
                for q in range(per):
                    out[at, places[q]] = jnp.where(fit, olds[q] + moved[q], olds[q]).astype(BF16)

    for j in range(AHEAD + 1):
        send_deltas(j)

    @pl.loop(0, levels)
    def _(level):
        for m in range(choices):
            def count(p, total):
                named = jnp.where(table[level, p] == m, 1.0, 0.0)
                wts[(level * n_path + p) * choices + m] = named
                return total + named

            counts[level * choices + m] = lax.fori_loop(0, n_path, count, jnp.float32(0.0))

    load_x.wait()

    @pl.loop(0, tokens // TILE)
    def _(i):
        at = pl.ds(pl.multiple_of(i * TILE, TILE), TILE)
        xf = out[at, :].astype(F32)
        scale = lax.rsqrt(jnp.mean(xf * xf, axis=1, keepdims=True) + 1e-06)
        nrm[z, at, :] = (xf * scale).astype(BF16)

    z_copy(nrm.at[z, top], nrm.at[z, top], ag_snd.at[0], ag_l.at[0], right)
    z_copy(nrm.at[z, low], nrm.at[z, low], ag_snd.at[0], ag_r.at[1], left)
    z_copy(nrm.at[z, low], nrm.at[z, low], ag_snd.at[0], ag_l.at[1], right)
    z_copy(nrm.at[z, top], nrm.at[z, top], ag_snd.at[0], ag_r.at[0], left)
    load_m.wait()

    @pl.loop(0, jobs + 5)
    def _(n):
        def when(low_job, job, high_job, *steps):
            @pl.when((job >= low_job) & (job < high_job))
            def _():
                for step in steps:
                    step()

        when(0, n - 2, jobs, lambda: step3(n - 2))

        def arrived():
            for t in range(2):
                wait_like(rec.at[n - 4, t], s_b.at[n - 4, t])

        when(0, n - 4, jobs, arrived)
        when(per_level, n - 4, jobs, lambda: rs_first(n - 4 - per_level))
        when(0, n - 1, jobs, lambda: step2(n - 1))
        when(0, n - 3, jobs, lambda: step5(n - 3))
        when(0, n, jobs, lambda: step1(n))
        @pl.when(n == 4)
        def _():
            wait_like(nrm.at[left, top], ag_l.at[0])
            z_copy(nrm.at[left, top], nrm.at[left, top], ag_snd.at[0], ag_f.at[0], right)
            wait_like(nrm.at[right, low], ag_r.at[1])
            z_copy(nrm.at[right, low], nrm.at[right, low], ag_snd.at[0], ag_f.at[1], left)

        when(per_level - 1, n - 4, per_level, first_projection)
        when(0, n - 2, jobs, lambda: step4(n - 2))
        when(AHEAD + 1, n + AHEAD, jobs, lambda: send_deltas(n + AHEAD))
        when(per_level, n - 4, jobs, lambda: rs_second(n - 4 - per_level))
        when(per_level, n - 5, jobs, lambda: rs_last(n - 5 - per_level))

    others = pl.ds(0, group - 1)
    wait_like(rec.at[:, :, others], o_a.at[0])
    wait_like(rec.at[:, :, others], o_b.at[0])
    wait_like(dense.at[:, :, pl.ds(0, 3)], o_bi.at[0])
    for j in range(jobs - SLOTS, jobs):
        wait_like(part.at[j % SLOTS], o_p.at[j])
    wait_like(nrm.at[pl.ds(0, 3)], rs_snd.at[0])


def per_device(path_table, master, momentum, deltas, activations):
    n_path = lax.axis_size("path")
    n_shard = lax.axis_size("shard")
    levels = deltas.shape[1]
    modules, rows, cols = master.shape
    choices = modules // levels
    tokens, width = activations.shape
    group = n_path // SIDE
    per_level = rows // TILE
    jobs = levels * per_level
    hbm = pl.BlockSpec(memory_space=pl.ANY)
    vmem = pl.BlockSpec(memory_space=pltpu.VMEM)
    smem = pl.BlockSpec(memory_space=pltpu.SMEM)
    dma = pltpu.SemaphoreType.DMA
    block = n_path * TILE
    wide = cols // 2
    return tuple(pl.pallas_call(
        kernel,
        out_shape=(
            pltpu.VMEM((modules, rows, cols), F32),
            pltpu.VMEM((tokens, width), BF16),
        ),
        in_specs=[smem, hbm, hbm, hbm, hbm],
        out_specs=(vmem, vmem),
        scratch_shapes=[
            pltpu.SMEM((levels * n_path * choices,), F32),
            pltpu.SMEM((modules,), F32),
            pltpu.VMEM((n_shard, tokens, width), BF16),
            pltpu.VMEM((SLOTS, choices, TILE, cols), F32),
            pltpu.VMEM((jobs, 2, group, SIDE, TILE, wide), BF16),
            pltpu.VMEM((SLOTS, 2, 3, choices, TILE, wide), BF16),
            pltpu.VMEM((jobs, 2, 2, choices // 2, TILE, wide), BF16),
            pltpu.VMEM((jobs, 2, 2, choices, TILE, wide), BF16),
            pltpu.VMEM((jobs, 2, SIDE, choices, TILE, wide), BF16),
            pltpu.VMEM((2, SIDE, choices, TILE, wide), BF16),
            pltpu.VMEM((SIDE, SIDE, 2, rows, cols), BF16),
            pltpu.VMEM((per_level, SIDE, SIDE, 2, TILE, cols), BF16),
            pltpu.VMEM((n_shard, tokens, cols), BF16),
            pltpu.VMEM((per_level, 2, tokens // 2, block), BF16),
            pltpu.VMEM((per_level, 2, tokens, block), BF16),
            dma((jobs, 2)), dma((jobs, 2, 2)), dma((jobs, 2, 2)), dma((jobs, 2)), dma((jobs, 2, 2)), dma((jobs, 2)),
            dma((1,)), dma((jobs,)), dma((1,)), dma((1,)),
            dma((1,)), dma((2,)), dma((2,)), dma((2,)),
            dma((1,)), dma((per_level, 2)), dma((per_level, 2)),
            dma((2,)), dma((SLOTS,)),
        ],
        compiler_params=pltpu.CompilerParams(
            collective_id=0, has_side_effects=True, vmem_limit_bytes=56 * 1024 * 1024
        ),
    )(
        path_table.T,
        master,
        momentum,
        deltas.reshape(levels, SIDE, SIDE, 2, rows, cols),
        activations,
    ))


def solution(mesh):
    placed = (
        P(),
        P(None, "path", "shard"),
        P(None, "path", "shard"),
        P("path", None, None, "shard"),
        P(("path", "shard"), None),
    )
    return jax.shard_map(
        per_device,
        mesh=mesh,
        in_specs=placed,
        out_specs=(P(None, "path", "shard"), P(("path", "shard"), None)),
        check_vma=False,
    )
```
